256 devices in a mesh: xb: 16 (over z, y_lo), fsdp: 16 (over x, y_hi, core).
Axes of the slice: x: 4, y: 4 (y_hi: 2, y_lo: 2; y = y_hi * 2 + y_lo), z: 8, core: 2. Of those that a mesh axis runs over, the one named last changes fastest.
Arguments:
- tokens: bfloat16 [256, 128, 2048], P(('xb', 'fsdp')), may hold values from -24 to 24
- query_weight: bfloat16 [2048, 2048], P('fsdp'), may hold values from -0.125 to 0.125
- current_keys: bfloat16 [256, 128, 2048], P(('xb', 'fsdp')), may hold values from -6 to 6
- current_values: bfloat16 [256, 128, 2048], P(('xb', 'fsdp')), may hold values from -6 to 6
- cache_keys: bfloat16 [256, 512, 2048], P(('xb', 'fsdp')), may hold values from -480 to 480
- cache_values: bfloat16 [256, 512, 2048], P(('xb', 'fsdp')), may hold values from -6 to 6
- cache_fill: int32 [256], P(('xb', 'fsdp')), may hold values from 1 to 512, as said below
- document_group: int32 [256], replicated, may hold values from 0 to 1
- attended_grad: bfloat16 [256, 128, 2048], P(('xb', 'fsdp')), may hold values from -6 to 6
Outputs:
- attended: bfloat16 [256, 128, 2048], P(('xb', 'fsdp'))
- tokens_grad: bfloat16 [256, 128, 2048], P(('xb', 'fsdp'))
- keys_grad: bfloat16 [256, 128, 2048], P(('xb', 'fsdp'))
- values_grad: bfloat16 [256, 128, 2048], P(('xb', 'fsdp'))
- weight_grad: float32 [2048, 2048], P('fsdp')
The draws below stay inside these ranges and needn't reach their ends.
Inputs may be any that keep to these rules, and one draw needn't show every extreme that they name: `cache_fill`: each document uses the first entries of its cache; some document uses all 512.
All inputs are finite; a program needn't handle non-finite values.
Results may differ from the reference program's by a relative error of at most 0.04.
Values may be sent and summed in bfloat16 or wider, within the bound.
No kernel may reach another device: no remote copies, remote signals or barrier semaphores. Data moves between devices by JAX's collectives and lax.ppermute only.
A program may use at most 128 MiB of HBM per device.

```python
import jax
import jax.numpy as jnp
from jax import lax

D = 2048
HEADS = 16
HEAD = 128
SEQ = 128
CACHE = 512
HD = 2048
DOCS = 256
N_XB = 16
N_FSDP = 16


def draw_cache_keys(key, part):
    key = jax.random.fold_in(key, 5)
    base = jnp.clip(jax.random.normal(key, (DOCS, CACHE, HEADS * HEAD), jnp.float32), -6.0, 6.0)
    return base.astype(jnp.bfloat16)


def draw_cache_fill(key, part):
    key = jax.random.fold_in(key, 7)
    fill_key, pick_key = jax.random.split(key)
    fills = jax.random.randint(fill_key, (DOCS,), 1, CACHE + 1, jnp.int32)
    chosen = jax.random.randint(pick_key, (), 0, DOCS, jnp.int32)
    return jnp.where(jnp.arange(DOCS, dtype=jnp.int32) == chosen, CACHE, fills).astype(jnp.int32)


def with_ends(entries, rng, least, high):
    longest = entries.shape.index(max(entries.shape))
    spots = []
    for shift in (0, 1):
        where = [jax.random.randint(jax.random.fold_in(rng, axis), (), 0, length) for axis, length in enumerate(entries.shape)]
        where[longest] = (where[longest] + shift) % entries.shape[longest]
        spots.append(tuple(where))
    return entries.at[spots[0]].set(least).at[spots[1]].set(high)


def spiked(array, key, source, target, blocks, factor):
    owner, partner = [(jnp.arange(array.shape[axis_at]) // (array.shape[axis_at] // blocks)).reshape([-1 if axis == axis_at else 1 for axis in range(array.ndim)]) for axis_at in (source, target)]
    chosen = jax.random.permutation(key, blocks)[partner]
    strong = (owner == chosen) | (owner == (partner + blocks // 2) % blocks)
    return jnp.where(strong, factor * array, array)


def levels(key, shape, pieces, least, high):
    def one(axis_at, blocks):
        steps = jax.random.uniform(jax.random.fold_in(jax.random.fold_in(key, 6), axis_at), (blocks,), jnp.float32, least / len(pieces), high / len(pieces))
        return jnp.repeat(jnp.exp(steps), shape[axis_at] // blocks).reshape((-1,) + (1,) * (len(shape) - axis_at - 1))

    loudness = one(*pieces[0])
    for cut in pieces[1:]:
        loudness = loudness * one(*cut)
    return loudness


def scatter_about(stream_key, extent, spread, reach, shards=(), held_as=jnp.bfloat16):
    factor_of = levels(stream_key, extent, shards, -0.22, 0.18) if shards else 1.0
    result = jax.random.normal(stream_key, extent, jnp.float32) * spread * factor_of
    return jnp.minimum(jnp.maximum(result, -reach), reach).astype(held_as)


def bell_draw_with(stream_key, extent, spread, reach, cuts, heavy, kind=jnp.bfloat16):
    entries = spread * jax.random.normal(stream_key, extent, jnp.float32)
    if cuts:
        entries = entries * levels(stream_key, extent, cuts, -0.22, 0.18)
    return jnp.clip(spiked(entries, jax.random.fold_in(stream_key, 3), *heavy), -reach, reach).astype(kind)


def setup_inputs(seed: int = 0) -> dict:
    key_list = jax.random.split(jax.random.key(seed), 10)
    return {
        "tokens": bell_draw_with(key_list[0], (DOCS, SEQ, D), 1.0, 24.0, ((0, 256),), (0, 2, 256, 6.0)),
        "query_weight": scatter_about(key_list[1], (D, HD), D ** -0.5, 0.125, ((0, 16),)),
        "current_keys": scatter_about(key_list[2], (DOCS, SEQ, HD), 1.0, 6.0, ((0, 256),)),
        "current_values": scatter_about(key_list[3], (DOCS, SEQ, HD), 1.0, 6.0, ((0, 256),)),
        "cache_keys": draw_cache_keys(jax.random.fold_in(key_list[9], 71), 0),
        "cache_values": scatter_about(key_list[5], (DOCS, CACHE, HD), 1.0, 6.0, ((0, 256),)),
        "cache_fill": draw_cache_fill(jax.random.fold_in(key_list[9], 71), 0),
        "document_group": with_ends(jax.random.randint(key_list[7], (DOCS,), 0, 2), jax.random.fold_in(key_list[7], 1), 0, 1).astype(jnp.int32),
        "attended_grad": scatter_about(key_list[8], (DOCS, SEQ, HD), 1.0, 6.0, ((0, 256),)),
    }


NEG = -1.0e30


def block_scores(query, key_rows):
    scaling = query.shape[-1] ** -0.5
    return jnp.einsum('the,khe->thk', query.astype(jnp.float32), key_rows.astype(jnp.float32)) * scaling


def block_forward(query, key_rows, value_rows, key_mask):
    scores = block_scores(query, key_rows)
    valid = key_mask[:, None, :]
    top_value = jnp.max(jnp.where(valid, scores, NEG), axis=-1)
    weights = jnp.where(valid, jnp.exp(scores - top_value[..., None]), 0.0).astype(jnp.bfloat16)
    totals = jnp.sum(weights.astype(jnp.float32), axis=-1)
    partial_sum = jnp.einsum('thk,khe->the', weights.astype(jnp.float32), value_rows.astype(jnp.float32))
    return top_value, totals, partial_sum, weights


def block_backward(weights, factor, grad_out, row_delta, key_rows, value_rows):
    scaling = key_rows.shape[-1] ** -0.5
    probs = weights.astype(jnp.float32) * factor[..., None]
    dprob = jnp.einsum('the,khe->thk', grad_out.astype(jnp.float32), value_rows.astype(jnp.float32))
    slope = (probs * (dprob - row_delta[..., None])).astype(jnp.bfloat16)
    query_part = jnp.einsum('thk,khe->the', slope.astype(jnp.float32), key_rows.astype(jnp.float32)) * scaling
    return probs, slope, query_part


def reference(tokens, query_weight, current_keys, current_values, cache_keys, cache_values, cache_fill, document_group, attended_grad):
    full_width = HEADS * HEAD
    grid_keys = current_keys.reshape(N_XB, N_FSDP, SEQ, full_width)
    grid_values = current_values.reshape(N_XB, N_FSDP, SEQ, full_width)
    grid_labels = document_group.reshape(N_XB, N_FSDP)
    positions = jnp.arange(SEQ)
    causal = positions[:, None] >= positions[None, :]

    def one_document(number):
        row_index = number // N_FSDP
        col_index = number % N_FSDP
        queries = jnp.dot(tokens[number], query_weight, preferred_element_type=jnp.float32).astype(jnp.bfloat16)
        query = queries.reshape(SEQ, HEADS, HEAD)
        own_keys = current_keys[number].reshape(SEQ, HEADS, HEAD)
        own_values = current_values[number].reshape(SEQ, HEADS, HEAD)
        peer_keys = grid_keys[:, col_index].reshape(N_XB * SEQ, HEADS, HEAD)
        peer_values = grid_values[:, col_index].reshape(N_XB * SEQ, HEADS, HEAD)
        labels = grid_labels[:, col_index]
        peer_valid = (labels == document_group[number]) & (jnp.arange(N_XB) != row_index)
        cross_mask = jnp.broadcast_to(jnp.repeat(peer_valid, SEQ)[None, :], (SEQ, N_XB * SEQ))
        stale_keys = cache_keys[number].reshape(CACHE, HEADS, HEAD)
        stale_values = cache_values[number].reshape(CACHE, HEADS, HEAD)
        stale_mask = jnp.broadcast_to((jnp.arange(CACHE) < cache_fill[number])[None, :], (SEQ, CACHE))
        local_fwd = block_forward(query, own_keys, own_values, causal)
        cross_fwd = block_forward(query, peer_keys, peer_values, cross_mask)
        stale_fwd = block_forward(query, stale_keys, stale_values, stale_mask)
        biggest = jnp.maximum(jnp.maximum(local_fwd[0], cross_fwd[0]), stale_fwd[0])
        local_share = jnp.exp(local_fwd[0] - biggest)
        cross_share = jnp.exp(cross_fwd[0] - biggest)
        stale_share = jnp.exp(stale_fwd[0] - biggest)
        norm_total = local_share * local_fwd[1] + cross_share * cross_fwd[1] + stale_share * stale_fwd[1]
        combined = local_share[..., None] * local_fwd[2] + cross_share[..., None] * cross_fwd[2] + stale_share[..., None] * stale_fwd[2]
        attended = (combined / norm_total[..., None]).astype(jnp.bfloat16)
        grad_out = attended_grad[number].reshape(SEQ, HEADS, HEAD)
        row_delta = jnp.sum(grad_out.astype(jnp.float32) * attended.astype(jnp.float32), axis=-1)
        local_bwd = block_backward(local_fwd[3], local_share / norm_total, grad_out, row_delta, own_keys, own_values)
        cross_bwd = block_backward(cross_fwd[3], cross_share / norm_total, grad_out, row_delta, peer_keys, peer_values)
        stale_bwd = block_backward(stale_fwd[3], stale_share / norm_total, grad_out, row_delta, stale_keys, stale_values)
        query_grad = (local_bwd[2] + cross_bwd[2] + stale_bwd[2]).astype(jnp.bfloat16).reshape(SEQ, full_width)
        scaling = HEAD ** -0.5
        keys_grad = (jnp.einsum('thk,the->khe', local_bwd[1].astype(jnp.float32), query.astype(jnp.float32)) * scaling).astype(jnp.bfloat16)
        local_prob = local_bwd[0].astype(jnp.bfloat16)
        values_grad = jnp.einsum('thk,the->khe', local_prob.astype(jnp.float32), grad_out.astype(jnp.float32)).astype(jnp.bfloat16)
        tokens_grad = jnp.dot(query_grad, query_weight.T, preferred_element_type=jnp.float32).astype(jnp.bfloat16)
        return (attended.reshape(SEQ, full_width), tokens_grad, keys_grad.reshape(SEQ, full_width),
                values_grad.reshape(SEQ, full_width), query_grad)

    attended, tokens_grad, keys_grad, values_grad, query_grad = lax.map(one_document, jnp.arange(DOCS, dtype=jnp.int32))
    weight_grad = jnp.dot(tokens.reshape(DOCS * SEQ, D).T, query_grad.reshape(DOCS * SEQ, full_width), preferred_element_type=jnp.float32)
    return attended, tokens_grad, keys_grad, values_grad, weight_grad
```

```python
import functools

import jax
import jax.numpy as jnp
from jax import lax
from jax.experimental import pallas as pl
from jax.experimental.pallas import tpu as pltpu
from jax.sharding import Mesh
from jax.sharding import PartitionSpec as P

HEADS = 16
HEAD = 128
SEQ = 128
NEG = -1e30
FLOOR = -1e29
SCALING = HEAD ** (-0.5)
LOG2E = 1.4426950408889634
XB = ("g", "q")
FS = ("x", "yh", "core")
BF = jnp.bfloat16
F32 = jnp.float32


def dot_nt(a, b):
    return lax.dot_general(a, b, (((1,), (1,)), ((), ())), preferred_element_type=F32)


def dot_nn(a, b):
    return lax.dot_general(a, b, (((1,), (0,)), ((), ())), preferred_element_type=F32)


def split3(x):
    hi = x.astype(BF)
    rest = x - hi.astype(F32)
    mid = rest.astype(BF)
    low = (rest - mid.astype(F32)).astype(BF)
    return hi, mid, low


def stat_rows(columns):
    lane = lax.broadcasted_iota(jnp.int32, (SEQ, SEQ), 1)
    tile = jnp.zeros((SEQ, SEQ), F32)
    for i, column in enumerate(columns):
        tile = jnp.where(lane == i, column, tile)
    return tile.T


def cross_kernel(q_ref, kvg_ref, g_ref, bias_ref, out_ref, k_s, v_s, kv_s):
    docs = kvg_ref.shape[0]

    @pl.when(pl.program_id(0) == 0)
    def _():
        for m in range(docs):
            k = kvg_ref[m, 0]
            v = kvg_ref[m, 1]
            k_s[m * SEQ : (m + 1) * SEQ, :] = k
            v_s[m * SEQ : (m + 1) * SEQ, :] = v
            kv_s[m * SEQ : (m + 1) * SEQ, :HEAD] = v
            kv_s[m * SEQ : (m + 1) * SEQ, HEAD:] = k

    for j in range(q_ref.shape[0]):
        q = q_ref[j]
        g = g_ref[j, 0]
        scores = dot_nt(q, k_s[...]) * (SCALING * LOG2E) + bias_ref[j]
        top = jnp.maximum(jnp.max(scores, axis=1, keepdims=True), FLOOR)
        weights = jnp.exp2(scores - top).astype(BF)
        weights32 = weights.astype(F32)
        total = jnp.sum(weights32, axis=1, keepdims=True)
        inverse = 1.0 / jnp.maximum(total, 0.5)
        both = dot_nn(weights, kv_s[...]) * inverse
        o = both[:, :HEAD]
        delta = jnp.sum(o * g.astype(F32), axis=1, keepdims=True)
        slope = (weights32 * (dot_nt(g, v_s[...]) - delta)).astype(BF)
        a = dot_nn(slope, k_s[...]) * inverse
        out_ref[j, 0:SEQ, :] = o.astype(BF)
        out_ref[j, SEQ : 2 * SEQ, :] = a.astype(BF)
        out_ref[j, 2 * SEQ : 3 * SEQ, :] = both[:, HEAD:].astype(BF)
        top = jnp.where(total > 0.0, top, NEG)
        rows = stat_rows([top, total, delta])[0:8, :]
        hi, mid, low = split3(rows)
        out_ref[j, 3 * SEQ : 3 * SEQ + 16, :] = jnp.concatenate(
            [hi.astype(F32), mid.astype(F32)], axis=0
        ).astype(BF)
        out_ref[j, 3 * SEQ + 16 : 3 * SEQ + 32, :] = jnp.concatenate(
            [low.astype(F32), jnp.zeros((8, SEQ), F32)], axis=0
        ).astype(BF)


def cross_attention(q_heads, kvg, bias):
    docs = q_heads.shape[0]
    step = 2
    return pl.pallas_call(
        cross_kernel,
        grid=(docs // step,),
        in_specs=[
            pl.BlockSpec((step, SEQ, HEAD), lambda i: (i, 0, 0)),
            pl.BlockSpec((docs, 2, SEQ, HEAD), lambda i: (0, 0, 0, 0)),
            pl.BlockSpec((step, 1, SEQ, HEAD), lambda i: (i, 2, 0, 0)),
            pl.BlockSpec((step, 1, docs * SEQ), lambda i: (i, 0, 0)),
        ],
        out_specs=pl.BlockSpec((step, 3 * SEQ + 32, HEAD), lambda i: (i, 0, 0)),
        out_shape=jax.ShapeDtypeStruct((docs, 3 * SEQ + 32, HEAD), BF),
        scratch_shapes=[
            pltpu.VMEM((docs * SEQ, HEAD), BF),
            pltpu.VMEM((docs * SEQ, HEAD), BF),
            pltpu.VMEM((docs * SEQ, 2 * HEAD), BF),
        ],
        compiler_params=pltpu.CompilerParams(vmem_limit_bytes=40 * 2**20),
        cost_estimate=pl.CostEstimate(
            flops=10 * docs * docs * SEQ * SEQ * HEAD,
            bytes_accessed=4 * 2**20,
            transcendentals=docs * docs * SEQ * SEQ,
        ),
        name="cross",
    )(q_heads, kvg, kvg, bias)


def own_kernel(fill_ref, q_ref, g_ref, ck_ref, cv_ref, lk_ref, lv_ref, o_ref, a_ref, b_ref, s_ref):
    q = q_ref[0]
    g = g_ref[0]
    cache = ck_ref.shape[1]
    entry = lax.broadcasted_iota(jnp.int32, (SEQ, cache), 1)
    row = lax.broadcasted_iota(jnp.int32, (SEQ, SEQ), 0)
    col = lax.broadcasted_iota(jnp.int32, (SEQ, SEQ), 1)
    stale = jnp.where(
        entry < fill_ref[0], dot_nt(q, ck_ref[0]) * (SCALING * LOG2E), NEG
    )
    local = jnp.where(col <= row, dot_nt(q, lk_ref[0]) * (SCALING * LOG2E), NEG)
    top = jnp.maximum(
        jnp.max(stale, axis=1, keepdims=True), jnp.max(local, axis=1, keepdims=True)
    )
    ws = jnp.exp2(stale - top).astype(BF)
    wl = jnp.exp2(local - top).astype(BF)
    ws32 = ws.astype(F32)
    wl32 = wl.astype(F32)
    total = jnp.sum(ws32, axis=1, keepdims=True) + jnp.sum(wl32, axis=1, keepdims=True)
    inverse = 1.0 / total
    o = (dot_nn(ws, cv_ref[0]) + dot_nn(wl, lv_ref[0])) * inverse
    b = (dot_nn(ws, ck_ref[0]) + dot_nn(wl, lk_ref[0])) * inverse
    delta = jnp.sum(o * g.astype(F32), axis=1, keepdims=True)
    ss = (ws32 * (dot_nt(g, cv_ref[0]) - delta)).astype(BF)
    sl = (wl32 * (dot_nt(g, lv_ref[0]) - delta)).astype(BF)
    o_ref[...] = o
    a_ref[...] = (dot_nn(ss, ck_ref[0]) + dot_nn(sl, lk_ref[0])) * inverse
    b_ref[...] = b
    s_ref[0] = stat_rows([top, total, delta])[0:8, :]


def own_attention(fill, q_own, grad, cache_k, cache_v, local_k, local_v):
    cache = cache_k.shape[1]
    width = HEADS * HEAD
    head_block = pl.BlockSpec((1, SEQ, HEAD), lambda h, f: (0, 0, h))
    cache_block = pl.BlockSpec((1, cache, HEAD), lambda h, f: (0, 0, h))
    out_block = pl.BlockSpec((SEQ, HEAD), lambda h, f: (0, h))
    return pl.pallas_call(
        own_kernel,
        grid_spec=pltpu.PrefetchScalarGridSpec(
            num_scalar_prefetch=1,
            grid=(HEADS,),
            in_specs=[
                pl.BlockSpec((1, SEQ, HEAD), lambda h, f: (h % 4, 0, h // 4)),
                head_block,
                cache_block,
                cache_block,
                head_block,
                head_block,
            ],
            out_specs=[
                out_block,
                out_block,
                out_block,
                pl.BlockSpec((1, 8, SEQ), lambda h, f: (h, 0, 0)),
            ],
        ),
        out_shape=[
            jax.ShapeDtypeStruct((SEQ, width), F32),
            jax.ShapeDtypeStruct((SEQ, width), F32),
            jax.ShapeDtypeStruct((SEQ, width), F32),
            jax.ShapeDtypeStruct((HEADS, 8, SEQ), F32),
        ],
        compiler_params=pltpu.CompilerParams(vmem_limit_bytes=24 * 2**20),
        cost_estimate=pl.CostEstimate(
            flops=10 * SEQ * (cache + SEQ) * width,
            bytes_accessed=9 * 2**20,
            transcendentals=SEQ * (cache + SEQ) * HEADS,
        ),
        name="own",
    )(fill, q_own, grad, cache_k, cache_v, local_k, local_v)


def combine_kernel(x_ref, o_ref, a_ref, b_ref, s_ref, g_ref, att_ref, qg_ref, t_ref):
    g = g_ref[0].astype(F32)
    packed = x_ref[0, 3 * SEQ : 3 * SEQ + 32, :].astype(F32)
    rows = packed[0:8] + packed[8:16] + packed[16:24]
    mine = s_ref[0]
    tile = jnp.concatenate([rows, mine, jnp.zeros((SEQ - 16, SEQ), F32)], axis=0).T
    x_top, x_total, x_delta = tile[:, 0:1], tile[:, 1:2], tile[:, 2:3]
    o_top, o_total, o_delta = tile[:, 8:9], tile[:, 9:10], tile[:, 10:11]
    big = jnp.maximum(x_top, o_top)
    x_share = jnp.exp2(x_top - big)
    o_share = jnp.exp2(o_top - big)
    inverse = 1.0 / (x_share * x_total + o_share * o_total)
    x_weight = x_share * x_total * inverse
    o_weight = o_share * o_total * inverse
    attended = (x_weight * x_ref[0, 0:SEQ, :].astype(F32) + o_weight * o_ref[...]).astype(BF)
    delta = jnp.sum(g * attended.astype(F32), axis=1, keepdims=True)
    grad = x_weight * (
        x_ref[0, SEQ : 2 * SEQ, :].astype(F32)
        + (x_delta - delta) * x_ref[0, 2 * SEQ : 3 * SEQ, :].astype(F32)
    ) + o_weight * (a_ref[...] + (o_delta - delta) * b_ref[...])
    att_ref[0] = attended
    qg_ref[0] = (grad * SCALING).astype(BF)
    t_ref[0] = stat_rows([o_top, o_share * inverse, delta])[0:8, :]


def combine(returned, o, a, b, stats, grad):
    width = HEADS * HEAD
    block = pl.BlockSpec((SEQ, HEAD), lambda h: (0, h))
    row_block = pl.BlockSpec((1, SEQ, HEAD), lambda h: (0, 0, h))
    stat_block = pl.BlockSpec((1, 8, SEQ), lambda h: (h, 0, 0))
    return pl.pallas_call(
        combine_kernel,
        grid=(HEADS,),
        in_specs=[
            pl.BlockSpec((1, 3 * SEQ + 32, HEAD), lambda h: (h, 0, 0)),
            block,
            block,
            block,
            stat_block,
            row_block,
        ],
        out_specs=[
            row_block,
            pl.BlockSpec((1, SEQ, HEAD), lambda h: (h % 4, 0, h // 4)),
            stat_block,
        ],
        out_shape=[
            jax.ShapeDtypeStruct((1, SEQ, width), BF),
            jax.ShapeDtypeStruct((4, SEQ, 4 * HEAD), BF),
            jax.ShapeDtypeStruct((HEADS, 8, SEQ), F32),
        ],
        cost_estimate=pl.CostEstimate(
            flops=20 * SEQ * width, bytes_accessed=6 * 2**20, transcendentals=0
        ),
        name="combine",
    )(returned, o, a, b, stats, grad)


def local_kernel(t_ref, q_ref, g_ref, lk_ref, lv_ref, kg_ref, vg_ref):
    q = q_ref[0]
    g = g_ref[0]
    top, factor, delta = t_ref[0, 0:1, :], t_ref[0, 1:2, :], t_ref[0, 2:3, :]
    key = lax.broadcasted_iota(jnp.int32, (SEQ, SEQ), 0)
    query = lax.broadcasted_iota(jnp.int32, (SEQ, SEQ), 1)
    scores = jnp.where(key <= query, dot_nt(lk_ref[0], q) * (SCALING * LOG2E), NEG)
    prob = jnp.exp2(scores - top).astype(BF).astype(F32) * factor
    slope = (prob * (dot_nt(lv_ref[0], g) - delta)).astype(BF)
    vg_ref[0] = dot_nn(prob.astype(BF), g).astype(BF)
    kg_ref[0] = (dot_nn(slope, q) * SCALING).astype(BF)


def local_grads(stats, q_own, grad, local_k, local_v):
    width = HEADS * HEAD
    row_block = pl.BlockSpec((1, SEQ, HEAD), lambda h: (0, 0, h))
    return pl.pallas_call(
        local_kernel,
        grid=(HEADS,),
        in_specs=[
            pl.BlockSpec((1, 8, SEQ), lambda h: (h, 0, 0)),
            pl.BlockSpec((1, SEQ, HEAD), lambda h: (h % 4, 0, h // 4)),
            row_block,
            row_block,
            row_block,
        ],
        out_specs=[row_block, row_block],
        out_shape=[
            jax.ShapeDtypeStruct((1, SEQ, width), BF),
            jax.ShapeDtypeStruct((1, SEQ, width), BF),
        ],
        cost_estimate=pl.CostEstimate(
            flops=8 * SEQ * SEQ * width,
            bytes_accessed=3 * 2**20,
            transcendentals=SEQ * SEQ * HEADS,
        ),
        name="local",
    )(stats, q_own, grad, local_k, local_v)


def a2a(x, axis):
    return lax.all_to_all(x, axis, 0, 0, tiled=True)


def spread(x, count):
    return jnp.broadcast_to(x[None], (count,) + x.shape)


def body(
    tokens,
    query_weight,
    current_keys,
    current_values,
    cache_keys,
    cache_values,
    cache_fill,
    document_group,
    attended_grad,
):
    q_index = lax.axis_index("q")
    g_index = lax.axis_index("g")
    col_index = lax.axis_index(FS)
    shard_rows = query_weight.shape[0]

    quarter = lax.dynamic_index_in_dim(
        query_weight.reshape(shard_rows, 4, 4, HEAD), q_index, axis=2, keepdims=False
    ).reshape(shard_rows, 4 * HEAD)
    weight = a2a(spread(quarter, 16), FS).reshape(16 * shard_rows, 4 * HEAD)
    tok = a2a(spread(tokens[0], 4), "q").reshape(4 * SEQ, -1)

    kvg = jnp.stack(
        [
            x[0].reshape(SEQ, HEADS, HEAD).transpose(1, 0, 2)
            for x in (current_keys, current_values, attended_grad)
        ],
        axis=1,
    )
    kvg = a2a(kvg, XB)

    queries = jnp.dot(tok, weight, preferred_element_type=F32).astype(BF)
    by_head = queries.reshape(4 * SEQ, 4, HEAD).transpose(1, 0, 2)
    q_heads = a2a(by_head, "g").reshape(16, SEQ, HEAD)
    q_own = a2a(queries.reshape(4, SEQ, 4 * HEAD), "q")

    labels = lax.dynamic_index_in_dim(
        document_group.reshape(16, 16), col_index, axis=1, keepdims=False
    )
    number = jnp.arange(16)
    valid = (labels[:, None] == labels[None, :]) & (number[:, None] != number[None, :])
    bias = jnp.repeat(jnp.where(valid, 0.0, NEG).astype(F32), SEQ, axis=1)[:, None, :]

    returned = a2a(cross_attention(q_heads, kvg, bias), XB)
    o, a, b, stats = own_attention(
        cache_fill, q_own, attended_grad, cache_keys, cache_values, current_keys, current_values
    )
    attended, query_grad, stats = combine(returned, o, a, b, stats, attended_grad)

    qg = a2a(query_grad, "q").reshape(4 * SEQ, 4 * HEAD)
    partial = lax.dot_general(
        tok, qg, (((0,), (0,)), ((), ())), preferred_element_type=F32
    ).astype(BF)
    pieces = a2a(partial.reshape(16, shard_rows, 4 * HEAD), FS)
    mine = jnp.sum(pieces.astype(F32), axis=0).astype(BF)

    tokens_part = dot_nt(qg, weight).astype(BF).reshape(4, SEQ, -1)
    tokens_grad = jnp.sum(a2a(tokens_part, "q").astype(F32), axis=0, keepdims=True).astype(BF)
    keys_grad, values_grad = local_grads(stats, q_own, attended_grad, current_keys, current_values)

    summed = jnp.sum(a2a(spread(mine, 4), "g").astype(F32), axis=0).astype(BF)
    columns = a2a(spread(summed, 4), "q")
    weight_grad = (
        columns.reshape(4, shard_rows, 4, HEAD)
        .transpose(1, 2, 0, 3)
        .reshape(shard_rows, HEADS * HEAD)
        .astype(F32)
    )
    return attended, tokens_grad, keys_grad, values_grad, weight_grad


def solution(mesh):
    grid = Mesh(mesh.devices.reshape(4, 4, 4, 2, 2), XB + FS)
    docs = P(XB + FS, None, None)
    in_specs = (docs, P(FS, None), docs, docs, docs, docs, P(XB + FS), P(), docs)
    out_specs = (docs, docs, docs, docs, P(FS, None))
    return jax.shard_map(body, mesh=grid, in_specs=in_specs, out_specs=out_specs, check_vma=False)
```

```python
import functools

import jax
import jax.numpy as jnp
from jax import lax
from jax.experimental import pallas as pl
from jax.experimental.pallas import tpu as pltpu
from jax.sharding import Mesh
from jax.sharding import PartitionSpec as P

HEADS = 16
HEAD = 128
SEQ = 128
NEG = -1e30
FLOOR = -1e29
SCALING = HEAD ** (-0.5)
LOG2E = 1.4426950408889634
XB = ("g", "q")
FS = ("x", "yh", "core")
BF = jnp.bfloat16
F32 = jnp.float32


def dot_nt(a, b):
    return lax.dot_general(a, b, (((1,), (1,)), ((), ())), preferred_element_type=F32)


def dot_nn(a, b):
    return lax.dot_general(a, b, (((1,), (0,)), ((), ())), preferred_element_type=F32)


def split3(x):
    hi = x.astype(BF)
    rest = x - hi.astype(F32)
    mid = rest.astype(BF)
    low = (rest - mid.astype(F32)).astype(BF)
    return hi, mid, low


def stat_rows(columns):
    lane = lax.broadcasted_iota(jnp.int32, (SEQ, SEQ), 1)
    tile = jnp.zeros((SEQ, SEQ), F32)
    for i, column in enumerate(columns):
        tile = jnp.where(lane == i, column, tile)
    return tile.T


def pack_rows(rows):
    hi, mid, low = split3(rows)
    blank = jnp.zeros((8, SEQ), F32)
    parts = [hi.astype(F32), mid.astype(F32), low.astype(F32), blank]
    return jnp.concatenate(parts, axis=0).astype(BF)


def unpack_rows(packed):
    x = packed.astype(F32)
    return x[0:8] + x[8:16] + x[16:24]


def cross_kernel(idx_ref, q_ref, kvg_ref, bias_ref, ab_ref, o_ref, k_s, v_s, kv_s, *, slots):
    docs = kvg_ref.shape[0]
    step = q_ref.shape[0]

    @pl.when(pl.program_id(0) == 0)
    def _():
        for m in range(docs):
            k = kvg_ref[m, 0]
            v = kvg_ref[m, 1]
            k_s[m * SEQ : (m + 1) * SEQ, :] = k
            v_s[m * SEQ : (m + 1) * SEQ, :] = v
            kv_s[m * SEQ : (m + 1) * SEQ, :HEAD] = v
            kv_s[m * SEQ : (m + 1) * SEQ, HEAD:] = k

    for j in range(step):
        place = pl.program_id(0) * step + j
        slot = jnp.where(place < 4, slots[0], slots[1])
        doc = 4 * ((idx_ref[0] + 4 - slot) % 4) + (idx_ref[1] ^ (place % 4))
        q = q_ref[j]
        g = kvg_ref[doc, 2]
        scores = dot_nt(q, k_s[...]) * (SCALING * LOG2E) + bias_ref[doc]
        top = jnp.maximum(jnp.max(scores, axis=1, keepdims=True), FLOOR)
        weights = jnp.exp2(scores - top).astype(BF)
        weights32 = weights.astype(F32)
        total = jnp.sum(weights32, axis=1, keepdims=True)
        inverse = 1.0 / jnp.maximum(total, 0.5)
        both = dot_nn(weights, kv_s[...]) * inverse
        o = both[:, :HEAD]
        delta = jnp.sum(o * g.astype(F32), axis=1, keepdims=True)
        slope = (weights32 * (dot_nt(g, v_s[...]) - delta)).astype(BF)
        a = dot_nn(slope, k_s[...]) * inverse
        top = jnp.where(total > 0.0, top, NEG)
        packed = pack_rows(stat_rows([top, total, delta])[0:8, :])
        ab_ref[j, 0:SEQ, :] = a.astype(BF)
        ab_ref[j, SEQ : 2 * SEQ, :] = both[:, HEAD:].astype(BF)
        ab_ref[j, 2 * SEQ : 2 * SEQ + 32, :] = packed
        o_ref[j, 0:SEQ, :] = o.astype(BF)
        o_ref[j, SEQ : SEQ + 32, :] = packed


def cross_attention(idx, q_heads, kvg, bias, slots):
    docs = kvg.shape[0]
    some = q_heads.shape[0]
    step = 2
    return pl.pallas_call(
        functools.partial(cross_kernel, slots=slots),
        grid_spec=pltpu.PrefetchScalarGridSpec(
            num_scalar_prefetch=1,
            grid=(some // step,),
            in_specs=[
                pl.BlockSpec((step, SEQ, HEAD), lambda i, x: (i, 0, 0)),
                pl.BlockSpec((docs, 3, SEQ, HEAD), lambda i, x: (0, 0, 0, 0)),
                pl.BlockSpec((docs, 1, docs * SEQ), lambda i, x: (0, 0, 0)),
            ],
            out_specs=[
                pl.BlockSpec((step, 2 * SEQ + 32, HEAD), lambda i, x: (i, 0, 0)),
                pl.BlockSpec((step, SEQ + 32, HEAD), lambda i, x: (i, 0, 0)),
            ],
            scratch_shapes=[
                pltpu.VMEM((docs * SEQ, HEAD), BF),
                pltpu.VMEM((docs * SEQ, HEAD), BF),
                pltpu.VMEM((docs * SEQ, 2 * HEAD), BF),
            ],
        ),
        out_shape=[
            jax.ShapeDtypeStruct((some, 2 * SEQ + 32, HEAD), BF),
            jax.ShapeDtypeStruct((some, SEQ + 32, HEAD), BF),
        ],
        compiler_params=pltpu.CompilerParams(vmem_limit_bytes=40 * 2**20),
        cost_estimate=pl.CostEstimate(
            flops=some * SEQ * SEQ, bytes_accessed=2**16, transcendentals=0
        ),
        name="cross",
    )(idx, q_heads, kvg, bias)


def by_heads_kernel(*refs):
    out_ref = refs[3]
    for c in range(4):
        for i in range(3):
            out_ref[c, i] = refs[i][0, :, c * HEAD : (c + 1) * HEAD]


def by_heads(*arrays):
    block = pl.BlockSpec((1, SEQ, 4 * HEAD), lambda i: (0, 0, i))
    return pl.pallas_call(
        by_heads_kernel,
        grid=(4,),
        in_specs=[block] * 3,
        out_specs=pl.BlockSpec((4, 3, SEQ, HEAD), lambda i: (i, 0, 0, 0)),
        out_shape=jax.ShapeDtypeStruct((HEADS, 3, SEQ, HEAD), BF),
        cost_estimate=pl.CostEstimate(flops=0, bytes_accessed=3 * 2**20, transcendentals=0),
        name="by_heads",
    )(*arrays)


def own_kernel(
    idx_ref, q_ref, g_ref, ck_ref, cv_ref, lk_ref, lv_ref, ab_ref, o_ref, s_ref
):
    cache = ck_ref.shape[1]
    entry = lax.broadcasted_iota(jnp.int32, (SEQ, cache), 1)
    row = lax.broadcasted_iota(jnp.int32, (SEQ, SEQ), 0)
    col = lax.broadcasted_iota(jnp.int32, (SEQ, SEQ), 1)
    for c in range(4):
        cols = slice(c * HEAD, (c + 1) * HEAD)
        k = idx_ref[1] ^ c
        q = q_ref[k]
        g = g_ref[0, :, cols]
        ck, cv = ck_ref[0, :, cols], cv_ref[0, :, cols]
        lk, lv = lk_ref[0, :, cols], lv_ref[0, :, cols]
        stale = jnp.where(entry < idx_ref[2], dot_nt(q, ck) * (SCALING * LOG2E), NEG)
        local = jnp.where(col <= row, dot_nt(q, lk) * (SCALING * LOG2E), NEG)
        top = jnp.maximum(
            jnp.max(stale, axis=1, keepdims=True), jnp.max(local, axis=1, keepdims=True)
        )
        ws = jnp.exp2(stale - top).astype(BF)
        wl = jnp.exp2(local - top).astype(BF)
        ws32 = ws.astype(F32)
        wl32 = wl.astype(F32)
        total = jnp.sum(ws32, axis=1, keepdims=True) + jnp.sum(wl32, axis=1, keepdims=True)
        inverse = 1.0 / total
        o = (dot_nn(ws, cv) + dot_nn(wl, lv)) * inverse
        b = (dot_nn(ws, ck) + dot_nn(wl, lk)) * inverse
        delta = jnp.sum(o * g.astype(F32), axis=1, keepdims=True)
        ss = (ws32 * (dot_nt(g, cv) - delta)).astype(BF)
        sl = (wl32 * (dot_nt(g, lv) - delta)).astype(BF)
        a = (dot_nn(ss, ck) + dot_nn(sl, lk)) * inverse
        rows = stat_rows([top, total, delta])[0:8, :]
        ab_ref[k, 0:SEQ, :] = a.astype(BF)
        ab_ref[k, SEQ : 2 * SEQ, :] = b.astype(BF)
        ab_ref[k, 2 * SEQ : 2 * SEQ + 32, :] = pack_rows(rows)
        o_ref[:, cols] = o
        s_ref[c] = rows


def own_attention(idx, q_own, grad, cache_k, cache_v, local_k, local_v):
    cache = cache_k.shape[1]
    width = HEADS * HEAD
    head_block = pl.BlockSpec((1, SEQ, 4 * HEAD), lambda j, x: (0, 0, (x[0] + j) % 4))
    cache_block = pl.BlockSpec((1, cache, 4 * HEAD), lambda j, x: (0, 0, (x[0] + j) % 4))
    return pl.pallas_call(
        own_kernel,
        grid_spec=pltpu.PrefetchScalarGridSpec(
            num_scalar_prefetch=1,
            grid=(4,),
            in_specs=[
                pl.BlockSpec((4, SEQ, HEAD), lambda j, x: (0, 0, j)),
                head_block,
                cache_block,
                cache_block,
                head_block,
                head_block,
            ],
            out_specs=[
                pl.BlockSpec((4, 2 * SEQ + 32, HEAD), lambda j, x: (0, 0, j)),
                pl.BlockSpec((SEQ, 4 * HEAD), lambda j, x: (0, (x[0] + j) % 4)),
                pl.BlockSpec((4, 8, SEQ), lambda j, x: ((x[0] + j) % 4, 0, 0)),
            ],
        ),
        out_shape=[
            jax.ShapeDtypeStruct((4, 2 * SEQ + 32, 4 * HEAD), BF),
            jax.ShapeDtypeStruct((SEQ, width), F32),
            jax.ShapeDtypeStruct((HEADS, 8, SEQ), F32),
        ],
        compiler_params=pltpu.CompilerParams(vmem_limit_bytes=24 * 2**20),
        cost_estimate=pl.CostEstimate(
            flops=cache * SEQ, bytes_accessed=2**16, transcendentals=0
        ),
        name="own",
    )(idx, q_own, grad, cache_k, cache_v, local_k, local_v)


def merge_rows(x_top, x_total, x_delta, o_top, o_total, o_delta):
    big = jnp.maximum(x_top, o_top)
    x_share = jnp.exp2(x_top - big)
    o_share = jnp.exp2(o_top - big)
    inverse = 1.0 / (x_share * x_total + o_share * o_total)
    x_weight = x_share * x_total * inverse
    o_weight = o_share * o_total * inverse
    delta = x_weight * x_delta + o_weight * o_delta
    return x_weight, o_weight, delta, o_share * inverse


def dest_kernel(*refs):
    x_refs, y_refs, qg_ref = refs[0:4], refs[4:8], refs[8]
    base = 2 * SEQ
    xs = [unpack_rows(x_refs[j][k, base : base + 32, :]) for k in range(4) for j in range(4)]
    ys = [
        unpack_rows(y_refs[k][base : base + 32, j * HEAD : (j + 1) * HEAD])
        for k in range(4)
        for j in range(4)
    ]
    x_stat = [jnp.concatenate([t[i : i + 1] for t in xs], axis=0) for i in range(3)]
    y_stat = [jnp.concatenate([t[i : i + 1] for t in ys], axis=0) for i in range(3)]
    x_weight, o_weight, delta, _ = merge_rows(*x_stat, *y_stat)
    rows = [
        x_weight * SCALING,
        x_weight * (x_stat[2] - delta) * SCALING,
        o_weight * SCALING,
        o_weight * (y_stat[2] - delta) * SCALING,
    ]
    tile = jnp.concatenate([*rows, jnp.zeros((SEQ - 64, SEQ), F32)], axis=0).T
    for k in range(4):
        for j in range(4):
            c = k * 4 + j
            cols = slice(j * HEAD, (j + 1) * HEAD)
            grad = (
                tile[:, c : c + 1] * x_refs[j][k, 0:SEQ, :].astype(F32)
                + tile[:, 16 + c : 17 + c] * x_refs[j][k, SEQ:base, :].astype(F32)
                + tile[:, 32 + c : 33 + c] * y_refs[k][0:SEQ, cols].astype(F32)
                + tile[:, 48 + c : 49 + c] * y_refs[k][SEQ:base, cols].astype(F32)
            )
            qg_ref[k * SEQ : (k + 1) * SEQ, cols] = grad.astype(BF)


def dest_combine(xs, ys):
    return pl.pallas_call(
        dest_kernel,
        out_shape=jax.ShapeDtypeStruct((4 * SEQ, 4 * HEAD), BF),
        compiler_params=pltpu.CompilerParams(vmem_limit_bytes=24 * 2**20),
        cost_estimate=pl.CostEstimate(
            flops=8 * 16 * SEQ * HEAD, bytes_accessed=3 * 2**20, transcendentals=0
        ),
        name="dest",
    )(*xs, *ys)


def finish_kernel(
    idx_ref, x_ref, o_ref, s_ref, q_ref, g_ref, lk_ref, lv_ref, att_ref, kg_ref, vg_ref
):
    key = lax.broadcasted_iota(jnp.int32, (SEQ, SEQ), 0)
    query = lax.broadcasted_iota(jnp.int32, (SEQ, SEQ), 1)
    for c in range(4):
        cols = slice(c * HEAD, (c + 1) * HEAD)
        k = idx_ref[1] ^ c
        q = q_ref[k]
        g = g_ref[0, :, cols]
        xr = unpack_rows(x_ref[k, 0, SEQ : SEQ + 32, :])
        yr = s_ref[c]
        x_weight, o_weight, delta, factor = merge_rows(
            xr[0:1], xr[1:2], xr[2:3], yr[0:1], yr[1:2], yr[2:3]
        )
        pair = jnp.concatenate([x_weight, o_weight, jnp.zeros((SEQ - 2, SEQ), F32)], axis=0).T
        att_ref[0, :, cols] = (
            pair[:, 0:1] * x_ref[k, 0, 0:SEQ, :].astype(F32) + pair[:, 1:2] * o_ref[:, cols]
        ).astype(BF)
        scores = dot_nt(lk_ref[0, :, cols], q) * (SCALING * LOG2E)
        scores = jnp.where(key <= query, scores, NEG)
        prob = jnp.exp2(scores - yr[0:1]).astype(BF).astype(F32) * factor
        slope = (prob * (dot_nt(lv_ref[0, :, cols], g) - delta)).astype(BF)
        vg_ref[0, :, cols] = dot_nn(prob.astype(BF), g).astype(BF)
        kg_ref[0, :, cols] = (dot_nn(slope, q) * SCALING).astype(BF)


def finish(idx, returned, o, stats, q_own, grad, local_k, local_v):
    width = HEADS * HEAD
    row_block = pl.BlockSpec((1, SEQ, 4 * HEAD), lambda i, x: (0, 0, i))
    return pl.pallas_call(
        finish_kernel,
        grid_spec=pltpu.PrefetchScalarGridSpec(
            num_scalar_prefetch=1,
            grid=(4,),
            in_specs=[
                pl.BlockSpec((4, 1, SEQ + 32, HEAD), lambda i, x: (0, (i + 4 - x[0]) % 4, 0, 0)),
                pl.BlockSpec((SEQ, 4 * HEAD), lambda i, x: (0, i)),
                pl.BlockSpec((4, 8, SEQ), lambda i, x: (i, 0, 0)),
                pl.BlockSpec((4, SEQ, HEAD), lambda i, x: (0, 0, (i + 4 - x[0]) % 4)),
                row_block,
                row_block,
                row_block,
            ],
            out_specs=[row_block, row_block, row_block],
        ),
        out_shape=[jax.ShapeDtypeStruct((1, SEQ, width), BF)] * 3,
        compiler_params=pltpu.CompilerParams(vmem_limit_bytes=24 * 2**20),
        cost_estimate=pl.CostEstimate(
            flops=10 * SEQ * SEQ * width,
            bytes_accessed=5 * 2**20,
            transcendentals=SEQ * SEQ * HEADS,
        ),
        name="finish",
    )(idx, returned, o, stats, q_own, grad, local_k, local_v)


def place_kernel(idx_ref, *refs):
    out_ref = refs[4]
    for k in range(4):
        for j in range(4):
            head = 4 * ((idx_ref[0] + j) % 4) + (idx_ref[1] ^ k)
            start = pl.multiple_of(head * HEAD, HEAD)
            out_ref[:, pl.ds(start, HEAD)] = refs[k][:, j * HEAD : (j + 1) * HEAD].astype(F32)


def place(idx, parts):
    rows = parts[0].shape[0]
    return pl.pallas_call(
        place_kernel,
        in_specs=[pl.BlockSpec(memory_space=pltpu.SMEM)] + [pl.BlockSpec()] * 4,
        out_shape=jax.ShapeDtypeStruct((rows, HEADS * HEAD), F32),
        cost_estimate=pl.CostEstimate(flops=0, bytes_accessed=2 * 2**20, transcendentals=0),
        name="place",
    )(idx, *parts)


def a2a(x, axis):
    return lax.all_to_all(x, axis, 0, 0, tiled=True)


def shift(x, axis, k):
    return lax.ppermute(x, axis, [(s, (s + k) % 4) for s in range(4)]) if k % 4 else x


def swap(x, axis, k):
    return lax.ppermute(x, axis, [(s, s ^ k) for s in range(4)]) if k else x


def in_order(mine, other, first, axis):
    return jnp.stack([jnp.where(first, mine, other), jnp.where(first, other, mine)], axis=axis)


def gather_shards(shard):
    x_index = lax.axis_index("x")
    slots = jnp.stack([shift(shard, "x", -k) for k in range(4)])
    slots = jnp.where(x_index % 2 == 1, jnp.roll(slots, 1, axis=0), slots)
    slots = jnp.where(x_index >= 2, jnp.roll(slots, 2, axis=0), slots)
    other = lax.ppermute(slots, "yh", [(0, 1), (1, 0)])
    slots = in_order(slots, other, lax.axis_index("yh") == 0, 1)
    other = lax.ppermute(slots, "core", [(0, 1), (1, 0)])
    slots = in_order(slots, other, lax.axis_index("core") == 0, 2)
    return slots.reshape(16 * shard.shape[0], -1)


def scatter_sum(partial):
    rows = partial.shape[0] // 16
    pairs = partial.reshape(8, 2, rows, -1)
    core = lax.axis_index("core")
    keep = lax.dynamic_index_in_dim(pairs, core, axis=1, keepdims=False)
    give = lax.dynamic_index_in_dim(pairs, 1 - core, axis=1, keepdims=False)
    got = lax.ppermute(give, "core", [(0, 1), (1, 0)])
    both = (keep.astype(F32) + got.astype(F32)).astype(BF)
    return jnp.sum(a2a(both, ("x", "yh")).astype(F32), axis=0), both


def body(
    tokens,
    query_weight,
    current_keys,
    current_values,
    cache_keys,
    cache_values,
    cache_fill,
    document_group,
    attended_grad,
):
    g_index = lax.axis_index("g")
    q_index = lax.axis_index("q")
    col_index = lax.axis_index(FS)
    idx = jnp.stack([g_index, q_index, cache_fill[0]]).astype(jnp.int32)

    pair = jnp.stack([tokens[0], swap(tokens[0], "q", 2)])
    far = swap(pair, "q", 1)
    quarter = jnp.concatenate(
        [
            lax.dynamic_slice_in_dim(
                query_weight, (4 * ((g_index + j) % 4) + q_index) * HEAD, HEAD, axis=1
            )
            for j in range(4)
        ],
        axis=1,
    )
    weight = gather_shards(quarter)

    kvg = by_heads(current_keys, current_values, attended_grad)
    kvg = a2a(kvg, XB)

    tok = jnp.concatenate([pair, far]).reshape(4 * SEQ, -1)
    queries = jnp.dot(tok, weight, preferred_element_type=F32).astype(BF)
    queries, kvg = lax.optimization_barrier((queries, kvg))
    queries = queries.reshape(2, 2, SEQ, -1).transpose(1, 0, 2, 3).reshape(4 * SEQ, -1)
    by_slot = [queries[:, j * HEAD : (j + 1) * HEAD] for j in range(4)]
    q_heads = [shift(by_slot[j], "g", j).reshape(4, SEQ, HEAD) for j in range(4)]
    q_own = jnp.stack([swap(queries[k * SEQ : (k + 1) * SEQ], "q", k) for k in range(4)])

    labels = lax.dynamic_index_in_dim(
        document_group.reshape(16, 16), col_index, axis=1, keepdims=False
    )
    number = jnp.arange(16)
    valid = (labels[:, None] == labels[None, :]) & (number[:, None] != number[None, :])
    bias = jnp.repeat(jnp.where(valid, 0.0, NEG).astype(F32), SEQ, axis=1)[:, None, :]

    ab, out = [None] * 4, [None] * 4
    halves = ((2, 0), (1, 3))
    two = [jnp.concatenate([q_heads[j] for j in slots]) for slots in halves]

    def cross_half(n):
        both, outs = cross_attention(idx, two[n], kvg, bias, halves[n])
        for i, j in enumerate(halves[n]):
            ab[j], out[j] = both[4 * i : 4 * i + 4], outs[4 * i : 4 * i + 4]
        return both

    q_own, _ = lax.optimization_barrier((q_own, cross_half(0)))
    own_ab, o, stats = own_attention(
        idx, q_own, attended_grad, cache_keys, cache_values, current_keys, current_values
    )
    two[1], stats = lax.optimization_barrier((two[1], stats))
    cross_half(1)
    xs = [shift(ab[j], "g", -j) for j in range(4)]
    own_ab, xs[2] = lax.optimization_barrier((own_ab, xs[2]))
    ys = [swap(own_ab[k], "q", k) for k in range(4)]
    qg = dest_combine(xs, ys)

    tok = tok.reshape(2, 2, SEQ, -1).transpose(1, 0, 2, 3).reshape(4 * SEQ, -1)
    partial = lax.dot_general(
        tok, qg, (((0,), (0,)), ((), ())), preferred_element_type=F32
    ).astype(BF)
    mine, sent = scatter_sum(partial)
    mine = mine.astype(BF)

    part = dot_nt(qg, weight).astype(BF).reshape(2, 2, SEQ, -1)
    swapped, mine = lax.optimization_barrier((swap(part[:, 1], "q", 1), mine))
    near = part[:, 0].astype(F32) + swapped.astype(F32)
    tokens_grad = near[0] + swap(near[1].astype(BF), "q", 2).astype(F32)
    tokens_grad = tokens_grad.astype(BF)[None]

    out, _ = lax.optimization_barrier((out, sent))
    over_g = [shift(out[j], "g", -j) for j in range(4)]
    over_g, _ = lax.optimization_barrier((over_g, mine))
    returned = jnp.stack(
        [swap(jnp.stack([over_g[j][k] for j in range(4)]), "q", k) for k in range(4)]
    )
    attended, keys_grad, values_grad = finish(
        idx, returned, o, stats, q_own, attended_grad, current_keys, current_values
    )

    summed = sum(
        jnp.roll(shift(mine, "g", k), -k * HEAD, axis=1).astype(F32) for k in range(4)
    ).astype(BF)
    weight_grad = place(idx, [swap(summed, "q", k) for k in range(4)])
    return attended, tokens_grad, keys_grad, values_grad, weight_grad


def solution(mesh):
    grid = Mesh(mesh.devices.reshape(4, 4, 4, 2, 2), XB + FS)
    docs = P(XB + FS, None, None)
    in_specs = (docs, P(FS, None), docs, docs, docs, docs, P(XB + FS), P(), docs)
    out_specs = (docs, docs, docs, docs, P(FS, None))
    return jax.shard_map(body, mesh=grid, in_specs=in_specs, out_specs=out_specs, check_vma=False)
```

```python
import functools

import jax
import jax.numpy as jnp
from jax import lax
from jax.experimental import pallas as pl
from jax.experimental.pallas import tpu as pltpu
from jax.sharding import Mesh
from jax.sharding import PartitionSpec as P

HEADS = 16
HEAD = 128
SEQ = 128
NEG = -1e30
FLOOR = -1e29
SCALING = HEAD ** (-0.5)
LOG2E = 1.4426950408889634
XB = ("g", "q")
FS = ("x", "yh", "core")
BF = jnp.bfloat16
F32 = jnp.float32


def dot_nt(a, b):
    return lax.dot_general(a, b, (((1,), (1,)), ((), ())), preferred_element_type=F32)


def dot_nn(a, b):
    return lax.dot_general(a, b, (((1,), (0,)), ((), ())), preferred_element_type=F32)


def split3(x):
    hi = x.astype(BF)
    rest = x - hi.astype(F32)
    mid = rest.astype(BF)
    low = (rest - mid.astype(F32)).astype(BF)
    return hi, mid, low


def stat_rows(columns):
    lane = lax.broadcasted_iota(jnp.int32, (SEQ, SEQ), 1)
    tile = jnp.zeros((SEQ, SEQ), F32)
    for i, column in enumerate(columns):
        tile = jnp.where(lane == i, column, tile)
    return tile.T


def pack_rows(rows):
    hi, mid, low = split3(rows)
    blank = jnp.zeros((8, SEQ), F32)
    parts = [hi.astype(F32), mid.astype(F32), low.astype(F32), blank]
    return jnp.concatenate(parts, axis=0).astype(BF)


def unpack_rows(packed):
    x = packed.astype(F32)
    return x[0:8] + x[8:16] + x[16:24]


def cross_kernel(idx_ref, q_ref, kvg_ref, bias_ref, ab_ref, o_ref, k_s, v_s, kv_s, *, slots):
    docs = kvg_ref.shape[0]
    step = q_ref.shape[0]

    @pl.when(pl.program_id(0) == 0)
    def _():
        for m in range(docs):
            k = kvg_ref[m, 0]
            v = kvg_ref[m, 1]
            k_s[m * SEQ : (m + 1) * SEQ, :] = k
            v_s[m * SEQ : (m + 1) * SEQ, :] = v
            kv_s[m * SEQ : (m + 1) * SEQ, :HEAD] = v
            kv_s[m * SEQ : (m + 1) * SEQ, HEAD:] = k

    first = pl.program_id(0) * step
    slot = jnp.where(first < 4, slots[0], slots[1])
    docs_at = [
        4 * ((idx_ref[0] + 4 - slot) % 4) + (idx_ref[1] ^ ((first + j) % 4)) for j in range(step)
    ]
    q = q_ref[...].reshape(step * SEQ, HEAD)
    g = jnp.concatenate([kvg_ref[doc, 2] for doc in docs_at], axis=0)
    scores = dot_nt(q, k_s[...]) * (SCALING * LOG2E)
    scores = jnp.concatenate(
        [scores[j * SEQ : (j + 1) * SEQ] + bias_ref[docs_at[j]] for j in range(step)], axis=0
    )
    top = jnp.maximum(jnp.max(scores, axis=1, keepdims=True), FLOOR)
    weights = jnp.exp2(scores - top).astype(BF)
    weights32 = weights.astype(F32)
    total = jnp.sum(weights32, axis=1, keepdims=True)
    inverse = 1.0 / jnp.maximum(total, 0.5)
    both = dot_nn(weights, kv_s[...]) * inverse
    o = both[:, :HEAD]
    delta = jnp.sum(o * g.astype(F32), axis=1, keepdims=True)
    slope = (weights32 * (dot_nt(g, v_s[...]) - delta)).astype(BF)
    a = dot_nn(slope, k_s[...]) * inverse
    top = jnp.where(total > 0.0, top, NEG)
    for j in range(step):
        rows = slice(j * SEQ, (j + 1) * SEQ)
        packed = pack_rows(stat_rows([top[rows], total[rows], delta[rows]])[0:8, :])
        ab_ref[j, 0:SEQ, :] = a[rows].astype(BF)
        ab_ref[j, SEQ : 2 * SEQ, :] = both[rows, HEAD:].astype(BF)
        ab_ref[j, 2 * SEQ : 2 * SEQ + 32, :] = packed
        o_ref[j, 0:SEQ, :] = o[rows].astype(BF)
        o_ref[j, SEQ : SEQ + 32, :] = packed


def cross_attention(idx, q_heads, kvg, bias, slots):
    docs = kvg.shape[0]
    some = q_heads.shape[0]
    step = 2
    return pl.pallas_call(
        functools.partial(cross_kernel, slots=slots),
        grid_spec=pltpu.PrefetchScalarGridSpec(
            num_scalar_prefetch=1,
            grid=(some // step,),
            in_specs=[
                pl.BlockSpec((step, SEQ, HEAD), lambda i, x: (i, 0, 0)),
                pl.BlockSpec((docs, 3, SEQ, HEAD), lambda i, x: (0, 0, 0, 0)),
                pl.BlockSpec((docs, 1, docs * SEQ), lambda i, x: (0, 0, 0)),
            ],
            out_specs=[
                pl.BlockSpec((step, 2 * SEQ + 32, HEAD), lambda i, x: (i, 0, 0)),
                pl.BlockSpec((step, SEQ + 32, HEAD), lambda i, x: (i, 0, 0)),
            ],
            scratch_shapes=[
                pltpu.VMEM((docs * SEQ, HEAD), BF),
                pltpu.VMEM((docs * SEQ, HEAD), BF),
                pltpu.VMEM((docs * SEQ, 2 * HEAD), BF),
            ],
        ),
        out_shape=[
            jax.ShapeDtypeStruct((some, 2 * SEQ + 32, HEAD), BF),
            jax.ShapeDtypeStruct((some, SEQ + 32, HEAD), BF),
        ],
        compiler_params=pltpu.CompilerParams(vmem_limit_bytes=40 * 2**20),
        cost_estimate=pl.CostEstimate(
            flops=some * SEQ * SEQ, bytes_accessed=2**16, transcendentals=0
        ),
        name="cross",
    )(idx, q_heads, kvg, bias)


def by_heads_kernel(*refs):
    out_ref = refs[3]
    for c in range(4):
        for i in range(3):
            out_ref[c, i] = refs[i][0, :, c * HEAD : (c + 1) * HEAD]


def by_heads(*arrays):
    block = pl.BlockSpec((1, SEQ, 4 * HEAD), lambda i: (0, 0, i))
    return pl.pallas_call(
        by_heads_kernel,
        grid=(4,),
        in_specs=[block] * 3,
        out_specs=pl.BlockSpec((4, 3, SEQ, HEAD), lambda i: (i, 0, 0, 0)),
        out_shape=jax.ShapeDtypeStruct((HEADS, 3, SEQ, HEAD), BF),
        cost_estimate=pl.CostEstimate(flops=0, bytes_accessed=3 * 2**20, transcendentals=0),
        name="by_heads",
    )(*arrays)


def own_kernel(
    idx_ref, q_ref, g_ref, ck_ref, cv_ref, lk_ref, lv_ref, ab_ref, o_ref, s_ref
):
    cache = ck_ref.shape[1]
    entry = lax.broadcasted_iota(jnp.int32, (SEQ, cache), 1)
    row = lax.broadcasted_iota(jnp.int32, (SEQ, SEQ), 0)
    col = lax.broadcasted_iota(jnp.int32, (SEQ, SEQ), 1)
    for c in range(4):
        cols = slice(c * HEAD, (c + 1) * HEAD)
        k = idx_ref[1] ^ c
        q = q_ref[k]
        g = g_ref[0, :, cols]
        ck, cv = ck_ref[0, :, cols], cv_ref[0, :, cols]
        lk, lv = lk_ref[0, :, cols], lv_ref[0, :, cols]
        stale = jnp.where(entry < idx_ref[2], dot_nt(q, ck) * (SCALING * LOG2E), NEG)
        local = jnp.where(col <= row, dot_nt(q, lk) * (SCALING * LOG2E), NEG)
        top = jnp.maximum(
            jnp.max(stale, axis=1, keepdims=True), jnp.max(local, axis=1, keepdims=True)
        )
        ws = jnp.exp2(stale - top).astype(BF)
        wl = jnp.exp2(local - top).astype(BF)
        ws32 = ws.astype(F32)
        wl32 = wl.astype(F32)
        total = jnp.sum(ws32, axis=1, keepdims=True) + jnp.sum(wl32, axis=1, keepdims=True)
        inverse = 1.0 / total
        o = (dot_nn(ws, cv) + dot_nn(wl, lv)) * inverse
        b = (dot_nn(ws, ck) + dot_nn(wl, lk)) * inverse
        delta = jnp.sum(o * g.astype(F32), axis=1, keepdims=True)
        ss = (ws32 * (dot_nt(g, cv) - delta)).astype(BF)
        sl = (wl32 * (dot_nt(g, lv) - delta)).astype(BF)
        a = (dot_nn(ss, ck) + dot_nn(sl, lk)) * inverse
        rows = stat_rows([top, total, delta])[0:8, :]
        ab_ref[k, 0:SEQ, :] = a.astype(BF)
        ab_ref[k, SEQ : 2 * SEQ, :] = b.astype(BF)
        ab_ref[k, 2 * SEQ : 2 * SEQ + 32, :] = pack_rows(rows)
        o_ref[:, cols] = o
        s_ref[c] = rows


def own_attention(idx, q_own, grad, cache_k, cache_v, local_k, local_v):
    cache = cache_k.shape[1]
    width = HEADS * HEAD
    head_block = pl.BlockSpec((1, SEQ, 4 * HEAD), lambda j, x: (0, 0, (x[0] + j) % 4))
    cache_block = pl.BlockSpec((1, cache, 4 * HEAD), lambda j, x: (0, 0, (x[0] + j) % 4))
    return pl.pallas_call(
        own_kernel,
        grid_spec=pltpu.PrefetchScalarGridSpec(
            num_scalar_prefetch=1,
            grid=(4,),
            in_specs=[
                pl.BlockSpec((4, SEQ, HEAD), lambda j, x: (0, 0, j)),
                head_block,
                cache_block,
                cache_block,
                head_block,
                head_block,
            ],
            out_specs=[
                pl.BlockSpec((4, 2 * SEQ + 32, HEAD), lambda j, x: (0, 0, j)),
                pl.BlockSpec((SEQ, 4 * HEAD), lambda j, x: (0, (x[0] + j) % 4)),
                pl.BlockSpec((4, 8, SEQ), lambda j, x: ((x[0] + j) % 4, 0, 0)),
            ],
        ),
        out_shape=[
            jax.ShapeDtypeStruct((4, 2 * SEQ + 32, 4 * HEAD), BF),
            jax.ShapeDtypeStruct((SEQ, width), F32),
            jax.ShapeDtypeStruct((HEADS, 8, SEQ), F32),
        ],
        compiler_params=pltpu.CompilerParams(vmem_limit_bytes=24 * 2**20),
        cost_estimate=pl.CostEstimate(
            flops=cache * SEQ, bytes_accessed=2**16, transcendentals=0
        ),
        name="own",
    )(idx, q_own, grad, cache_k, cache_v, local_k, local_v)


def merge_rows(x_top, x_total, x_delta, o_top, o_total, o_delta):
    big = jnp.maximum(x_top, o_top)
    x_share = jnp.exp2(x_top - big)
    o_share = jnp.exp2(o_top - big)
    inverse = 1.0 / (x_share * x_total + o_share * o_total)
    x_weight = x_share * x_total * inverse
    o_weight = o_share * o_total * inverse
    delta = x_weight * x_delta + o_weight * o_delta
    return x_weight, o_weight, delta, o_share * inverse


def dest_kernel(*refs):
    x_refs, y_refs, qg_ref = refs[0:4], refs[4:8], refs[8]
    base = 2 * SEQ
    xs = [unpack_rows(x_refs[j][k, base : base + 32, :]) for k in range(4) for j in range(4)]
    ys = [
        unpack_rows(y_refs[k][base : base + 32, j * HEAD : (j + 1) * HEAD])
        for k in range(4)
        for j in range(4)
    ]
    x_stat = [jnp.concatenate([t[i : i + 1] for t in xs], axis=0) for i in range(3)]
    y_stat = [jnp.concatenate([t[i : i + 1] for t in ys], axis=0) for i in range(3)]
    x_weight, o_weight, delta, _ = merge_rows(*x_stat, *y_stat)
    rows = [
        x_weight * SCALING,
        x_weight * (x_stat[2] - delta) * SCALING,
        o_weight * SCALING,
        o_weight * (y_stat[2] - delta) * SCALING,
    ]
    tile = jnp.concatenate([*rows, jnp.zeros((SEQ - 64, SEQ), F32)], axis=0).T
    for k in range(4):
        for j in range(4):
            c = k * 4 + j
            cols = slice(j * HEAD, (j + 1) * HEAD)
            grad = (
                tile[:, c : c + 1] * x_refs[j][k, 0:SEQ, :].astype(F32)
                + tile[:, 16 + c : 17 + c] * x_refs[j][k, SEQ:base, :].astype(F32)
                + tile[:, 32 + c : 33 + c] * y_refs[k][0:SEQ, cols].astype(F32)
                + tile[:, 48 + c : 49 + c] * y_refs[k][SEQ:base, cols].astype(F32)
            )
            qg_ref[k * SEQ : (k + 1) * SEQ, cols] = grad.astype(BF)


def dest_combine(xs, ys):
    return pl.pallas_call(
        dest_kernel,
        out_shape=jax.ShapeDtypeStruct((4 * SEQ, 4 * HEAD), BF),
        compiler_params=pltpu.CompilerParams(vmem_limit_bytes=24 * 2**20),
        cost_estimate=pl.CostEstimate(
            flops=8 * 16 * SEQ * HEAD, bytes_accessed=3 * 2**20, transcendentals=0
        ),
        name="dest",
    )(*xs, *ys)


def finish_kernel(
    idx_ref, x_ref, o_ref, s_ref, q_ref, g_ref, lk_ref, lv_ref, att_ref, kg_ref, vg_ref
):
    key = lax.broadcasted_iota(jnp.int32, (SEQ, SEQ), 0)
    query = lax.broadcasted_iota(jnp.int32, (SEQ, SEQ), 1)
    for c in range(4):
        cols = slice(c * HEAD, (c + 1) * HEAD)
        k = idx_ref[1] ^ c
        q = q_ref[k]
        g = g_ref[0, :, cols]
        xr = unpack_rows(x_ref[k, 0, SEQ : SEQ + 32, :])
        yr = s_ref[c]
        x_weight, o_weight, delta, factor = merge_rows(
            xr[0:1], xr[1:2], xr[2:3], yr[0:1], yr[1:2], yr[2:3]
        )
        pair = jnp.concatenate([x_weight, o_weight, jnp.zeros((SEQ - 2, SEQ), F32)], axis=0).T
        att_ref[0, :, cols] = (
            pair[:, 0:1] * x_ref[k, 0, 0:SEQ, :].astype(F32) + pair[:, 1:2] * o_ref[:, cols]
        ).astype(BF)
        scores = dot_nt(lk_ref[0, :, cols], q) * (SCALING * LOG2E)
        scores = jnp.where(key <= query, scores, NEG)
        prob = jnp.exp2(scores - yr[0:1]).astype(BF).astype(F32) * factor
        slope = (prob * (dot_nt(lv_ref[0, :, cols], g) - delta)).astype(BF)
        vg_ref[0, :, cols] = dot_nn(prob.astype(BF), g).astype(BF)
        kg_ref[0, :, cols] = (dot_nn(slope, q) * SCALING).astype(BF)


def finish(idx, returned, o, stats, q_own, grad, local_k, local_v):
    width = HEADS * HEAD
    row_block = pl.BlockSpec((1, SEQ, 4 * HEAD), lambda i, x: (0, 0, i))
    return pl.pallas_call(
        finish_kernel,
        grid_spec=pltpu.PrefetchScalarGridSpec(
            num_scalar_prefetch=1,
            grid=(4,),
            in_specs=[
                pl.BlockSpec((4, 1, SEQ + 32, HEAD), lambda i, x: (0, (i + 4 - x[0]) % 4, 0, 0)),
                pl.BlockSpec((SEQ, 4 * HEAD), lambda i, x: (0, i)),
                pl.BlockSpec((4, 8, SEQ), lambda i, x: (i, 0, 0)),
                pl.BlockSpec((4, SEQ, HEAD), lambda i, x: (0, 0, (i + 4 - x[0]) % 4)),
                row_block,
                row_block,
                row_block,
            ],
            out_specs=[row_block, row_block, row_block],
        ),
        out_shape=[jax.ShapeDtypeStruct((1, SEQ, width), BF)] * 3,
        compiler_params=pltpu.CompilerParams(vmem_limit_bytes=24 * 2**20),
        cost_estimate=pl.CostEstimate(
            flops=10 * SEQ * SEQ * width,
            bytes_accessed=5 * 2**20,
            transcendentals=SEQ * SEQ * HEADS,
        ),
        name="finish",
    )(idx, returned, o, stats, q_own, grad, local_k, local_v)


def place_kernel(idx_ref, *refs):
    out_ref = refs[4]
    for k in range(4):
        for j in range(4):
            head = 4 * ((idx_ref[0] + j) % 4) + (idx_ref[1] ^ k)
            start = pl.multiple_of(head * HEAD, HEAD)
            out_ref[:, pl.ds(start, HEAD)] = refs[k][:, j * HEAD : (j + 1) * HEAD].astype(F32)


def place(idx, parts):
    rows = parts[0].shape[0]
    return pl.pallas_call(
        place_kernel,
        in_specs=[pl.BlockSpec(memory_space=pltpu.SMEM)] + [pl.BlockSpec()] * 4,
        out_shape=jax.ShapeDtypeStruct((rows, HEADS * HEAD), F32),
        cost_estimate=pl.CostEstimate(flops=0, bytes_accessed=2 * 2**20, transcendentals=0),
        name="place",
    )(idx, *parts)


def a2a(x, axis):
    return lax.all_to_all(x, axis, 0, 0, tiled=True)


def shift(x, axis, k):
    return lax.ppermute(x, axis, [(s, (s + k) % 4) for s in range(4)]) if k % 4 else x


def swap(x, axis, k):
    return lax.ppermute(x, axis, [(s, s ^ k) for s in range(4)]) if k else x


def in_order(mine, other, first, axis):
    return jnp.stack([jnp.where(first, mine, other), jnp.where(first, other, mine)], axis=axis)


def gather_shards(shard):
    x_index = lax.axis_index("x")
    slots = jnp.stack([shift(shard, "x", -k) for k in range(4)])
    slots = jnp.where(x_index % 2 == 1, jnp.roll(slots, 1, axis=0), slots)
    slots = jnp.where(x_index >= 2, jnp.roll(slots, 2, axis=0), slots)
    other = lax.ppermute(slots, "yh", [(0, 1), (1, 0)])
    slots = in_order(slots, other, lax.axis_index("yh") == 0, 1)
    other = lax.ppermute(slots, "core", [(0, 1), (1, 0)])
    slots = in_order(slots, other, lax.axis_index("core") == 0, 2)
    return slots.reshape(16 * shard.shape[0], -1)


def scatter_sum(partial):
    rows = partial.shape[0] // 16
    pairs = partial.reshape(8, 2, rows, -1)
    core = lax.axis_index("core")
    keep = lax.dynamic_index_in_dim(pairs, core, axis=1, keepdims=False)
    give = lax.dynamic_index_in_dim(pairs, 1 - core, axis=1, keepdims=False)
    got = lax.ppermute(give, "core", [(0, 1), (1, 0)])
    both = (keep.astype(F32) + got.astype(F32)).astype(BF)
    return jnp.sum(a2a(both, ("x", "yh")).astype(F32), axis=0), both


def body(
    tokens,
    query_weight,
    current_keys,
    current_values,
    cache_keys,
    cache_values,
    cache_fill,
    document_group,
    attended_grad,
):
    g_index = lax.axis_index("g")
    q_index = lax.axis_index("q")
    col_index = lax.axis_index(FS)
    idx = jnp.stack([g_index, q_index, cache_fill[0]]).astype(jnp.int32)

    half = tokens.shape[2] // 2
    left, right = tokens[0, :, :half], tokens[0, :, half:]
    kvg = by_heads(current_keys, current_values, attended_grad)
    left2, right1 = swap(left, "q", 2), swap(right, "q", 1)
    left1, right2 = swap(left, "q", 1), swap(right, "q", 2)
    left1, left2, right1, right2, kvg = lax.optimization_barrier(
        (left1, left2, right1, right2, kvg)
    )
    left3, right3 = swap(left2, "q", 1), swap(right1, "q", 2)
    quarter = jnp.concatenate(
        [
            lax.dynamic_slice_in_dim(
                query_weight, (4 * ((g_index + j) % 4) + q_index) * HEAD, HEAD, axis=1
            )
            for j in range(4)
        ],
        axis=1,
    )
    weight = gather_shards(quarter)

    kvg = a2a(kvg, XB)

    tok = jnp.concatenate(
        [
            jnp.concatenate([left, left1, left2, left3]),
            jnp.concatenate([right, right1, right2, right3]),
        ],
        axis=1,
    )
    queries = jnp.dot(tok, weight, preferred_element_type=F32).astype(BF)
    queries, kvg = lax.optimization_barrier((queries, kvg))
    by_slot = [queries[:, j * HEAD : (j + 1) * HEAD] for j in range(4)]
    q_heads = [shift(by_slot[j], "g", j).reshape(4, SEQ, HEAD) for j in range(4)]
    q_own = jnp.stack([swap(queries[k * SEQ : (k + 1) * SEQ], "q", k) for k in range(4)])

    labels = lax.dynamic_index_in_dim(
        document_group.reshape(16, 16), col_index, axis=1, keepdims=False
    )
    number = jnp.arange(16)
    valid = (labels[:, None] == labels[None, :]) & (number[:, None] != number[None, :])
    bias = jnp.repeat(jnp.where(valid, 0.0, NEG).astype(F32), SEQ, axis=1)[:, None, :]

    ab, out = [None] * 4, [None] * 4
    halves = ((2, 0), (1, 3))
    two = [jnp.concatenate([q_heads[j] for j in slots]) for slots in halves]

    def cross_half(n):
        both, outs = cross_attention(idx, two[n], kvg, bias, halves[n])
        for i, j in enumerate(halves[n]):
            ab[j], out[j] = both[4 * i : 4 * i + 4], outs[4 * i : 4 * i + 4]
        return both

    q_own, _ = lax.optimization_barrier((q_own, cross_half(0)))
    up, down = shift(ab[2][:2], "g", -1), shift(ab[2][2:], "g", 1)
    own_ab, o, stats = own_attention(
        idx, q_own, attended_grad, cache_keys, cache_values, current_keys, current_values
    )
    two[1], stats, up, down = lax.optimization_barrier((two[1], stats, up, down))
    up, down = shift(up, "g", -1), shift(down, "g", 1)
    xs = [ab[0], None, jnp.concatenate([up, down]), None]
    ys = [swap(own_ab[k], "q", k) for k in range(4)]
    cross_half(1)
    xs[1], xs[3] = shift(ab[1], "g", -1), shift(ab[3], "g", -3)
    qg = dest_combine(xs, ys)

    partial = lax.dot_general(
        tok, qg, (((0,), (0,)), ((), ())), preferred_element_type=F32
    ).astype(BF)
    mine, sent = scatter_sum(partial)
    mine = mine.astype(BF)

    part = dot_nt(qg, weight).astype(BF).reshape(2, 2, SEQ, -1)
    swapped, mine = lax.optimization_barrier((swap(part[:, 1], "q", 1), mine))
    near = part[:, 0].astype(F32) + swapped.astype(F32)
    tokens_grad = near[0] + swap(near[1].astype(BF), "q", 2).astype(F32)
    tokens_grad = tokens_grad.astype(BF)[None]

    out, _ = lax.optimization_barrier((out, sent))
    over_g = [shift(out[j], "g", -j) for j in range(4)]
    over_g, _ = lax.optimization_barrier((over_g, mine))
    returned = jnp.stack(
        [swap(jnp.stack([over_g[j][k] for j in range(4)]), "q", k) for k in range(4)]
    )
    attended, keys_grad, values_grad = finish(
        idx, returned, o, stats, q_own, attended_grad, current_keys, current_values
    )

    summed = sum(
        jnp.roll(shift(mine, "g", k), -k * HEAD, axis=1).astype(F32) for k in range(4)
    ).astype(BF)
    weight_grad = place(idx, [swap(summed, "q", k) for k in range(4)])
    return attended, tokens_grad, keys_grad, values_grad, weight_grad


def solution(mesh):
    grid = Mesh(mesh.devices.reshape(4, 4, 4, 2, 2), XB + FS)
    docs = P(XB + FS, None, None)
    in_specs = (docs, P(FS, None), docs, docs, docs, docs, P(XB + FS), P(), docs)
    out_specs = (docs, docs, docs, docs, P(FS, None))
    return jax.shard_map(body, mesh=grid, in_specs=in_specs, out_specs=out_specs, check_vma=False)
```

```python
import functools

import jax
import jax.numpy as jnp
from jax import lax
from jax.experimental import pallas as pl
from jax.experimental.pallas import tpu as pltpu
from jax.sharding import Mesh
from jax.sharding import PartitionSpec as P

HEADS = 16
HEAD = 128
SEQ = 128
NEG = -1e30
FLOOR = -1e29
SCALING = HEAD ** (-0.5)
LOG2E = 1.4426950408889634
XB = ("g", "q")
FS = ("x", "yh", "core")
BF = jnp.bfloat16
F32 = jnp.float32


def dot_nt(a, b):
    return lax.dot_general(a, b, (((1,), (1,)), ((), ())), preferred_element_type=F32)


def dot_nn(a, b):
    return lax.dot_general(a, b, (((1,), (0,)), ((), ())), preferred_element_type=F32)


def split3(x):
    hi = x.astype(BF)
    rest = x - hi.astype(F32)
    mid = rest.astype(BF)
    low = (rest - mid.astype(F32)).astype(BF)
    return hi, mid, low


def stat_rows(columns):
    lane = lax.broadcasted_iota(jnp.int32, (SEQ, SEQ), 1)
    tile = jnp.zeros((SEQ, SEQ), F32)
    for i, column in enumerate(columns):
        tile = jnp.where(lane == i, column, tile)
    return tile.T


def pack_rows(rows):
    hi, mid, low = split3(rows)
    blank = jnp.zeros((8, SEQ), F32)
    parts = [hi.astype(F32), mid.astype(F32), low.astype(F32), blank]
    return jnp.concatenate(parts, axis=0).astype(BF)


def unpack_rows(packed):
    x = packed.astype(F32)
    return x[0:8] + x[8:16] + x[16:24]


def cross_kernel(idx_ref, q_ref, kvg_ref, bias_ref, ab_ref, o_ref, k_s, v_s, kv_s, *, slots):
    docs = kvg_ref.shape[0]
    step = q_ref.shape[0]

    @pl.when(pl.program_id(0) == 0)
    def _():
        for m in range(docs):
            k = kvg_ref[m, 0]
            v = kvg_ref[m, 1]
            k_s[m * SEQ : (m + 1) * SEQ, :] = k
            v_s[m * SEQ : (m + 1) * SEQ, :] = v
            kv_s[m * SEQ : (m + 1) * SEQ, :HEAD] = v
            kv_s[m * SEQ : (m + 1) * SEQ, HEAD:] = k

    first = pl.program_id(0) * step
    slot = jnp.where(first < 4, slots[0], slots[1])
    docs_at = [
        4 * ((idx_ref[0] + 4 - slot) % 4) + (idx_ref[1] ^ ((first + j) % 4)) for j in range(step)
    ]
    q = q_ref[...].reshape(step * SEQ, HEAD)
    g = jnp.concatenate([kvg_ref[doc, 2] for doc in docs_at], axis=0)
    scores = dot_nt(q, k_s[...]) * (SCALING * LOG2E)
    scores = jnp.concatenate(
        [scores[j * SEQ : (j + 1) * SEQ] + bias_ref[docs_at[j]] for j in range(step)], axis=0
    )
    top = jnp.maximum(jnp.max(scores, axis=1, keepdims=True), FLOOR)
    weights = jnp.exp2(scores - top).astype(BF)
    weights32 = weights.astype(F32)
    total = jnp.sum(weights32, axis=1, keepdims=True)
    inverse = 1.0 / jnp.maximum(total, 0.5)
    both = dot_nn(weights, kv_s[...]) * inverse
    o = both[:, :HEAD]
    delta = jnp.sum(o * g.astype(F32), axis=1, keepdims=True)
    slope = (weights32 * (dot_nt(g, v_s[...]) - delta)).astype(BF)
    a = dot_nn(slope, k_s[...]) * inverse
    top = jnp.where(total > 0.0, top, NEG)
    for j in range(step):
        rows = slice(j * SEQ, (j + 1) * SEQ)
        packed = pack_rows(stat_rows([top[rows], total[rows], delta[rows]])[0:8, :])
        ab_ref[j, 0:SEQ, :] = a[rows].astype(BF)
        ab_ref[j, SEQ : 2 * SEQ, :] = both[rows, HEAD:].astype(BF)
        ab_ref[j, 2 * SEQ : 2 * SEQ + 32, :] = packed
        o_ref[j, 0:SEQ, :] = o[rows].astype(BF)
        o_ref[j, SEQ : SEQ + 32, :] = packed


def cross_attention(idx, q_heads, kvg, bias, slots):
    docs = kvg.shape[0]
    some = q_heads.shape[0]
    step = 2
    return pl.pallas_call(
        functools.partial(cross_kernel, slots=slots),
        grid_spec=pltpu.PrefetchScalarGridSpec(
            num_scalar_prefetch=1,
            grid=(some // step,),
            in_specs=[
                pl.BlockSpec((step, SEQ, HEAD), lambda i, x: (i, 0, 0)),
                pl.BlockSpec((docs, 3, SEQ, HEAD), lambda i, x: (0, 0, 0, 0)),
                pl.BlockSpec((docs, 1, docs * SEQ), lambda i, x: (0, 0, 0)),
            ],
            out_specs=[
                pl.BlockSpec((step, 2 * SEQ + 32, HEAD), lambda i, x: (i, 0, 0)),
                pl.BlockSpec((step, SEQ + 32, HEAD), lambda i, x: (i, 0, 0)),
            ],
            scratch_shapes=[
                pltpu.VMEM((docs * SEQ, HEAD), BF),
                pltpu.VMEM((docs * SEQ, HEAD), BF),
                pltpu.VMEM((docs * SEQ, 2 * HEAD), BF),
            ],
        ),
        out_shape=[
            jax.ShapeDtypeStruct((some, 2 * SEQ + 32, HEAD), BF),
            jax.ShapeDtypeStruct((some, SEQ + 32, HEAD), BF),
        ],
        compiler_params=pltpu.CompilerParams(vmem_limit_bytes=40 * 2**20),
        cost_estimate=pl.CostEstimate(
            flops=some * SEQ * SEQ, bytes_accessed=2**16, transcendentals=0
        ),
        name="cross",
    )(idx, q_heads, kvg, bias)


def by_heads_kernel(*refs):
    out_ref = refs[3]
    for c in range(4):
        for i in range(3):
            out_ref[c, i] = refs[i][0, :, c * HEAD : (c + 1) * HEAD]


def by_heads(*arrays):
    block = pl.BlockSpec((1, SEQ, 4 * HEAD), lambda i: (0, 0, i))
    return pl.pallas_call(
        by_heads_kernel,
        grid=(4,),
        in_specs=[block] * 3,
        out_specs=pl.BlockSpec((4, 3, SEQ, HEAD), lambda i: (i, 0, 0, 0)),
        out_shape=jax.ShapeDtypeStruct((HEADS, 3, SEQ, HEAD), BF),
        cost_estimate=pl.CostEstimate(flops=0, bytes_accessed=3 * 2**20, transcendentals=0),
        name="by_heads",
    )(*arrays)


def own_kernel(
    idx_ref, q_ref, g_ref, ck_ref, cv_ref, lk_ref, lv_ref, ab_ref, o_ref, s_ref
):
    cache = ck_ref.shape[1]
    entry = lax.broadcasted_iota(jnp.int32, (SEQ, cache), 1)
    row = lax.broadcasted_iota(jnp.int32, (SEQ, SEQ), 0)
    col = lax.broadcasted_iota(jnp.int32, (SEQ, SEQ), 1)
    for c in range(4):
        cols = slice(c * HEAD, (c + 1) * HEAD)
        k = idx_ref[1] ^ c
        q = q_ref[k]
        g = g_ref[0, :, cols]
        ck, cv = ck_ref[0, :, cols], cv_ref[0, :, cols]
        lk, lv = lk_ref[0, :, cols], lv_ref[0, :, cols]
        stale = jnp.where(entry < idx_ref[2], dot_nt(q, ck) * (SCALING * LOG2E), NEG)
        local = jnp.where(col <= row, dot_nt(q, lk) * (SCALING * LOG2E), NEG)
        top = jnp.maximum(
            jnp.max(stale, axis=1, keepdims=True), jnp.max(local, axis=1, keepdims=True)
        )
        ws = jnp.exp2(stale - top).astype(BF)
        wl = jnp.exp2(local - top).astype(BF)
        ws32 = ws.astype(F32)
        wl32 = wl.astype(F32)
        total = jnp.sum(ws32, axis=1, keepdims=True) + jnp.sum(wl32, axis=1, keepdims=True)
        inverse = 1.0 / total
        o = (dot_nn(ws, cv) + dot_nn(wl, lv)) * inverse
        b = (dot_nn(ws, ck) + dot_nn(wl, lk)) * inverse
        delta = jnp.sum(o * g.astype(F32), axis=1, keepdims=True)
        ss = (ws32 * (dot_nt(g, cv) - delta)).astype(BF)
        sl = (wl32 * (dot_nt(g, lv) - delta)).astype(BF)
        a = (dot_nn(ss, ck) + dot_nn(sl, lk)) * inverse
        rows = stat_rows([top, total, delta])[0:8, :]
        ab_ref[k, 0:SEQ, :] = a.astype(BF)
        ab_ref[k, SEQ : 2 * SEQ, :] = b.astype(BF)
        ab_ref[k, 2 * SEQ : 2 * SEQ + 32, :] = pack_rows(rows)
        o_ref[:, cols] = o
        s_ref[c] = rows


def own_attention(idx, q_own, grad, cache_k, cache_v, local_k, local_v):
    cache = cache_k.shape[1]
    width = HEADS * HEAD
    head_block = pl.BlockSpec((1, SEQ, 4 * HEAD), lambda j, x: (0, 0, (x[0] + j) % 4))
    cache_block = pl.BlockSpec((1, cache, 4 * HEAD), lambda j, x: (0, 0, (x[0] + j) % 4))
    return pl.pallas_call(
        own_kernel,
        grid_spec=pltpu.PrefetchScalarGridSpec(
            num_scalar_prefetch=1,
            grid=(4,),
            in_specs=[
                pl.BlockSpec((4, SEQ, HEAD), lambda j, x: (0, 0, j)),
                head_block,
                cache_block,
                cache_block,
                head_block,
                head_block,
            ],
            out_specs=[
                pl.BlockSpec((4, 2 * SEQ + 32, HEAD), lambda j, x: (0, 0, j)),
                pl.BlockSpec((SEQ, 4 * HEAD), lambda j, x: (0, (x[0] + j) % 4)),
                pl.BlockSpec((4, 8, SEQ), lambda j, x: ((x[0] + j) % 4, 0, 0)),
            ],
        ),
        out_shape=[
            jax.ShapeDtypeStruct((4, 2 * SEQ + 32, 4 * HEAD), BF),
            jax.ShapeDtypeStruct((SEQ, width), F32),
            jax.ShapeDtypeStruct((HEADS, 8, SEQ), F32),
        ],
        compiler_params=pltpu.CompilerParams(vmem_limit_bytes=24 * 2**20),
        cost_estimate=pl.CostEstimate(
            flops=cache * SEQ, bytes_accessed=2**16, transcendentals=0
        ),
        name="own",
    )(idx, q_own, grad, cache_k, cache_v, local_k, local_v)


def merge_rows(x_top, x_total, x_delta, o_top, o_total, o_delta):
    big = jnp.maximum(x_top, o_top)
    x_share = jnp.exp2(x_top - big)
    o_share = jnp.exp2(o_top - big)
    inverse = 1.0 / (x_share * x_total + o_share * o_total)
    x_weight = x_share * x_total * inverse
    o_weight = o_share * o_total * inverse
    delta = x_weight * x_delta + o_weight * o_delta
    return x_weight, o_weight, delta, o_share * inverse


def dest_kernel(*refs):
    x_refs, y_refs, qg_ref = refs[0:4], refs[4:8], refs[8]
    base = 2 * SEQ
    xs = [unpack_rows(x_refs[j][k, base : base + 32, :]) for k in range(4) for j in range(4)]
    ys = [
        unpack_rows(y_refs[k][base : base + 32, j * HEAD : (j + 1) * HEAD])
        for k in range(4)
        for j in range(4)
    ]
    x_stat = [jnp.concatenate([t[i : i + 1] for t in xs], axis=0) for i in range(3)]
    y_stat = [jnp.concatenate([t[i : i + 1] for t in ys], axis=0) for i in range(3)]
    x_weight, o_weight, delta, _ = merge_rows(*x_stat, *y_stat)
    rows = [
        x_weight * SCALING,
        x_weight * (x_stat[2] - delta) * SCALING,
        o_weight * SCALING,
        o_weight * (y_stat[2] - delta) * SCALING,
    ]
    tile = jnp.concatenate([*rows, jnp.zeros((SEQ - 64, SEQ), F32)], axis=0).T
    for k in range(4):
        for j in range(4):
            c = k * 4 + j
            cols = slice(j * HEAD, (j + 1) * HEAD)
            grad = (
                tile[:, c : c + 1] * x_refs[j][k, 0:SEQ, :].astype(F32)
                + tile[:, 16 + c : 17 + c] * x_refs[j][k, SEQ:base, :].astype(F32)
                + tile[:, 32 + c : 33 + c] * y_refs[k][0:SEQ, cols].astype(F32)
                + tile[:, 48 + c : 49 + c] * y_refs[k][SEQ:base, cols].astype(F32)
            )
            qg_ref[k * SEQ : (k + 1) * SEQ, cols] = grad.astype(BF)


def dest_combine(xs, ys):
    return pl.pallas_call(
        dest_kernel,
        out_shape=jax.ShapeDtypeStruct((4 * SEQ, 4 * HEAD), BF),
        compiler_params=pltpu.CompilerParams(vmem_limit_bytes=24 * 2**20),
        cost_estimate=pl.CostEstimate(
            flops=8 * 16 * SEQ * HEAD, bytes_accessed=3 * 2**20, transcendentals=0
        ),
        name="dest",
    )(*xs, *ys)


def finish_kernel(
    idx_ref, x_ref, o_ref, s_ref, q_ref, g_ref, lk_ref, lv_ref, att_ref, kg_ref, vg_ref
):
    key = lax.broadcasted_iota(jnp.int32, (SEQ, SEQ), 0)
    query = lax.broadcasted_iota(jnp.int32, (SEQ, SEQ), 1)
    for c in range(4):
        cols = slice(c * HEAD, (c + 1) * HEAD)
        k = idx_ref[1] ^ c
        q = q_ref[k]
        g = g_ref[0, :, cols]
        xr = unpack_rows(x_ref[k, 0, SEQ : SEQ + 32, :])
        yr = s_ref[c]
        x_weight, o_weight, delta, factor = merge_rows(
            xr[0:1], xr[1:2], xr[2:3], yr[0:1], yr[1:2], yr[2:3]
        )
        pair = jnp.concatenate([x_weight, o_weight, jnp.zeros((SEQ - 2, SEQ), F32)], axis=0).T
        att_ref[0, :, cols] = (
            pair[:, 0:1] * x_ref[k, 0, 0:SEQ, :].astype(F32) + pair[:, 1:2] * o_ref[:, cols]
        ).astype(BF)
        scores = dot_nt(lk_ref[0, :, cols], q) * (SCALING * LOG2E)
        scores = jnp.where(key <= query, scores, NEG)
        prob = jnp.exp2(scores - yr[0:1]).astype(BF).astype(F32) * factor
        slope = (prob * (dot_nt(lv_ref[0, :, cols], g) - delta)).astype(BF)
        vg_ref[0, :, cols] = dot_nn(prob.astype(BF), g).astype(BF)
        kg_ref[0, :, cols] = (dot_nn(slope, q) * SCALING).astype(BF)


def finish(idx, returned, o, stats, q_own, grad, local_k, local_v):
    width = HEADS * HEAD
    row_block = pl.BlockSpec((1, SEQ, 4 * HEAD), lambda i, x: (0, 0, i))
    return pl.pallas_call(
        finish_kernel,
        grid_spec=pltpu.PrefetchScalarGridSpec(
            num_scalar_prefetch=1,
            grid=(4,),
            in_specs=[
                pl.BlockSpec((4, 1, SEQ + 32, HEAD), lambda i, x: (0, (i + 4 - x[0]) % 4, 0, 0)),
                pl.BlockSpec((SEQ, 4 * HEAD), lambda i, x: (0, i)),
                pl.BlockSpec((4, 8, SEQ), lambda i, x: (i, 0, 0)),
                pl.BlockSpec((4, SEQ, HEAD), lambda i, x: (0, 0, (i + 4 - x[0]) % 4)),
                row_block,
                row_block,
                row_block,
            ],
            out_specs=[row_block, row_block, row_block],
        ),
        out_shape=[jax.ShapeDtypeStruct((1, SEQ, width), BF)] * 3,
        compiler_params=pltpu.CompilerParams(vmem_limit_bytes=24 * 2**20),
        cost_estimate=pl.CostEstimate(
            flops=10 * SEQ * SEQ * width,
            bytes_accessed=5 * 2**20,
            transcendentals=SEQ * SEQ * HEADS,
        ),
        name="finish",
    )(idx, returned, o, stats, q_own, grad, local_k, local_v)


def place_kernel(idx_ref, *refs):
    out_ref = refs[4]
    for k in range(4):
        for j in range(4):
            head = 4 * ((idx_ref[0] + j) % 4) + (idx_ref[1] ^ k)
            start = pl.multiple_of(head * HEAD, HEAD)
            out_ref[:, pl.ds(start, HEAD)] = refs[k][:, j * HEAD : (j + 1) * HEAD].astype(F32)


def place(idx, parts):
    rows = parts[0].shape[0]
    return pl.pallas_call(
        place_kernel,
        in_specs=[pl.BlockSpec(memory_space=pltpu.SMEM)] + [pl.BlockSpec()] * 4,
        out_shape=jax.ShapeDtypeStruct((rows, HEADS * HEAD), F32),
        cost_estimate=pl.CostEstimate(flops=0, bytes_accessed=2 * 2**20, transcendentals=0),
        name="place",
    )(idx, *parts)


def a2a(x, axis):
    return lax.all_to_all(x, axis, 0, 0, tiled=True)


def shift(x, axis, k):
    return lax.ppermute(x, axis, [(s, (s + k) % 4) for s in range(4)]) if k % 4 else x


def swap(x, axis, k):
    return lax.ppermute(x, axis, [(s, s ^ k) for s in range(4)]) if k else x


def in_order(mine, other, first, axis):
    return jnp.stack([jnp.where(first, mine, other), jnp.where(first, other, mine)], axis=axis)


def gather_shards(shard, tok1, tok2):
    x_index = lax.axis_index("x")
    slots = jnp.stack([shift(shard, "x", -k) for k in range(4)])
    slots = jnp.where(x_index % 2 == 1, jnp.roll(slots, 1, axis=0), slots)
    slots = jnp.where(x_index >= 2, jnp.roll(slots, 2, axis=0), slots)
    slots, tok1, tok2 = lax.optimization_barrier((slots, tok1, tok2))
    tok3 = swap(tok2, "q", 1)
    other = lax.ppermute(slots, "yh", [(0, 1), (1, 0)])
    slots = in_order(slots, other, lax.axis_index("yh") == 0, 1)
    slots, tok3 = lax.optimization_barrier((slots, tok3))
    other = lax.ppermute(slots, "core", [(0, 1), (1, 0)])
    slots = in_order(slots, other, lax.axis_index("core") == 0, 2)
    return slots.reshape(16 * shard.shape[0], -1), tok1, tok2, tok3


def body(
    tokens,
    query_weight,
    current_keys,
    current_values,
    cache_keys,
    cache_values,
    cache_fill,
    document_group,
    attended_grad,
):
    g_index = lax.axis_index("g")
    q_index = lax.axis_index("q")
    col_index = lax.axis_index(FS)
    idx = jnp.stack([g_index, q_index, cache_fill[0]]).astype(jnp.int32)

    own_tok = tokens[0]
    tok2, tok1 = swap(own_tok, "q", 2), swap(own_tok, "q", 1)
    kvg = by_heads(current_keys, current_values, attended_grad)
    quarter = jnp.concatenate(
        [
            lax.dynamic_slice_in_dim(
                query_weight, (4 * ((g_index + j) % 4) + q_index) * HEAD, HEAD, axis=1
            )
            for j in range(4)
        ],
        axis=1,
    )
    weight, tok1, tok2, tok3 = gather_shards(quarter, tok1, tok2)

    kvg = a2a(kvg, XB)

    tok = jnp.concatenate([own_tok, tok1, tok2, tok3])
    queries = jnp.dot(tok, weight, preferred_element_type=F32).astype(BF)
    queries, kvg = lax.optimization_barrier((queries, kvg))
    by_slot = [queries[:, j * HEAD : (j + 1) * HEAD] for j in range(4)]
    q_heads = [shift(by_slot[j], "g", j).reshape(4, SEQ, HEAD) for j in range(4)]
    q_own = jnp.stack([swap(queries[k * SEQ : (k + 1) * SEQ], "q", k) for k in range(4)])

    labels = lax.dynamic_index_in_dim(
        document_group.reshape(16, 16), col_index, axis=1, keepdims=False
    )
    number = jnp.arange(16)
    valid = (labels[:, None] == labels[None, :]) & (number[:, None] != number[None, :])
    bias = jnp.repeat(jnp.where(valid, 0.0, NEG).astype(F32), SEQ, axis=1)[:, None, :]

    ab, out = [None] * 4, [None] * 4
    halves = ((2, 0), (1, 3))
    two = [jnp.concatenate([q_heads[j] for j in slots]) for slots in halves]

    def cross_half(n):
        both, outs = cross_attention(idx, two[n], kvg, bias, halves[n])
        for i, j in enumerate(halves[n]):
            ab[j], out[j] = both[4 * i : 4 * i + 4], outs[4 * i : 4 * i + 4]
        return both

    q_own, _ = lax.optimization_barrier((q_own, cross_half(0)))
    up, down = shift(ab[2][:2], "g", -1), shift(ab[2][2:], "g", 1)
    own_ab, o, stats = own_attention(
        idx, q_own, attended_grad, cache_keys, cache_values, current_keys, current_values
    )
    two[1], stats, up, down = lax.optimization_barrier((two[1], stats, up, down))
    up, down = shift(up, "g", -1), shift(down, "g", 1)
    xs = [ab[0], None, jnp.concatenate([up, down]), None]
    ys = [swap(own_ab[k], "q", k) for k in range(4)]
    cross_half(1)
    xs[1], xs[3] = shift(ab[1], "g", -1), shift(ab[3], "g", -3)
    qg = dest_combine(xs, ys)

    partial = lax.dot_general(
        tok, qg, (((0,), (0,)), ((), ())), preferred_element_type=F32
    ).astype(BF)
    pieces = a2a(partial.reshape(16, query_weight.shape[0], 4 * HEAD), FS)
    mine = jnp.sum(pieces.astype(F32), axis=0).astype(BF)

    part = dot_nt(qg, weight).astype(BF).reshape(2, 2, SEQ, -1)
    swapped, mine = lax.optimization_barrier((swap(part[:, 1], "q", 1), mine))
    near = part[:, 0].astype(F32) + swapped.astype(F32)
    tokens_grad = near[0] + swap(near[1].astype(BF), "q", 2).astype(F32)
    tokens_grad = tokens_grad.astype(BF)[None]

    out, _ = lax.optimization_barrier((out, partial))
    over_g = [shift(out[j], "g", -j) for j in range(4)]
    over_g, _ = lax.optimization_barrier((over_g, mine))
    returned = jnp.stack(
        [swap(jnp.stack([over_g[j][k] for j in range(4)]), "q", k) for k in range(4)]
    )
    attended, keys_grad, values_grad = finish(
        idx, returned, o, stats, q_own, attended_grad, current_keys, current_values
    )

    summed = sum(
        jnp.roll(shift(mine, "g", k), -k * HEAD, axis=1).astype(F32) for k in range(4)
    ).astype(BF)
    weight_grad = place(idx, [swap(summed, "q", k) for k in range(4)])
    return attended, tokens_grad, keys_grad, values_grad, weight_grad


def solution(mesh):
    grid = Mesh(mesh.devices.reshape(4, 4, 4, 2, 2), XB + FS)
    docs = P(XB + FS, None, None)
    in_specs = (docs, P(FS, None), docs, docs, docs, docs, P(XB + FS), P(), docs)
    out_specs = (docs, docs, docs, docs, P(FS, None))
    return jax.shard_map(body, mesh=grid, in_specs=in_specs, out_specs=out_specs, check_vma=False)
```

```python
import functools

import jax
import jax.numpy as jnp
from jax import lax
from jax.experimental import pallas as pl
from jax.experimental.pallas import tpu as pltpu
from jax.sharding import Mesh
from jax.sharding import PartitionSpec as P

HEADS = 16
HEAD = 128
SEQ = 128
NEG = -1e30
FLOOR = -1e29
SCALING = HEAD ** (-0.5)
LOG2E = 1.4426950408889634
XB = ("g", "q")
FS = ("x", "yh", "core")
BF = jnp.bfloat16
F32 = jnp.float32


def dot_nt(a, b):
    return lax.dot_general(a, b, (((1,), (1,)), ((), ())), preferred_element_type=F32)


def dot_nn(a, b):
    return lax.dot_general(a, b, (((1,), (0,)), ((), ())), preferred_element_type=F32)


def split3(x):
    hi = x.astype(BF)
    rest = x - hi.astype(F32)
    mid = rest.astype(BF)
    low = (rest - mid.astype(F32)).astype(BF)
    return hi, mid, low


def stat_rows(columns):
    lane = lax.broadcasted_iota(jnp.int32, (SEQ, SEQ), 1)
    tile = jnp.zeros((SEQ, SEQ), F32)
    for i, column in enumerate(columns):
        tile = jnp.where(lane == i, column, tile)
    return tile.T


def pack_rows(rows):
    hi, mid, low = split3(rows)
    blank = jnp.zeros((8, SEQ), F32)
    parts = [hi.astype(F32), mid.astype(F32), low.astype(F32), blank]
    return jnp.concatenate(parts, axis=0).astype(BF)


def unpack_rows(packed):
    x = packed.astype(F32)
    return x[0:8] + x[8:16] + x[16:24]


def cross_kernel(idx_ref, q_ref, kvg_ref, bias_ref, ab_ref, o_ref, k_s, v_s, kv_s, *, slots):
    docs = kvg_ref.shape[0]
    step = q_ref.shape[0]

    @pl.when(pl.program_id(0) == 0)
    def _():
        for m in range(docs):
            k = kvg_ref[m, 0]
            v = kvg_ref[m, 1]
            k_s[m * SEQ : (m + 1) * SEQ, :] = k
            v_s[m * SEQ : (m + 1) * SEQ, :] = v
            kv_s[m * SEQ : (m + 1) * SEQ, :HEAD] = v
            kv_s[m * SEQ : (m + 1) * SEQ, HEAD:] = k

    first = pl.program_id(0) * step
    slot = jnp.where(first < 4, slots[0], slots[1])
    docs_at = [
        4 * ((idx_ref[0] + 4 - slot) % 4) + (idx_ref[1] ^ ((first + j) % 4)) for j in range(step)
    ]
    q = q_ref[...].reshape(step * SEQ, HEAD)
    g = jnp.concatenate([kvg_ref[doc, 2] for doc in docs_at], axis=0)
    scores = dot_nt(q, k_s[...]) * (SCALING * LOG2E)
    scores = jnp.concatenate(
        [scores[j * SEQ : (j + 1) * SEQ] + bias_ref[docs_at[j]] for j in range(step)], axis=0
    )
    top = jnp.maximum(jnp.max(scores, axis=1, keepdims=True), FLOOR)
    weights = jnp.exp2(scores - top).astype(BF)
    weights32 = weights.astype(F32)
    total = jnp.sum(weights32, axis=1, keepdims=True)
    inverse = 1.0 / jnp.maximum(total, 0.5)
    both = dot_nn(weights, kv_s[...]) * inverse
    o = both[:, :HEAD]
    delta = jnp.sum(o * g.astype(F32), axis=1, keepdims=True)
    slope = (weights32 * (dot_nt(g, v_s[...]) - delta)).astype(BF)
    a = dot_nn(slope, k_s[...]) * inverse
    top = jnp.where(total > 0.0, top, NEG)
    for j in range(step):
        rows = slice(j * SEQ, (j + 1) * SEQ)
        packed = pack_rows(stat_rows([top[rows], total[rows], delta[rows]])[0:8, :])
        ab_ref[j, 0:SEQ, :] = a[rows].astype(BF)
        ab_ref[j, SEQ : 2 * SEQ, :] = both[rows, HEAD:].astype(BF)
        ab_ref[j, 2 * SEQ : 2 * SEQ + 32, :] = packed
        o_ref[j, 0:SEQ, :] = o[rows].astype(BF)
        o_ref[j, SEQ : SEQ + 32, :] = packed


def cross_attention(idx, q_heads, kvg, bias, slots):
    docs = kvg.shape[0]
    some = q_heads.shape[0]
    step = 2
    return pl.pallas_call(
        functools.partial(cross_kernel, slots=slots),
        grid_spec=pltpu.PrefetchScalarGridSpec(
            num_scalar_prefetch=1,
            grid=(some // step,),
            in_specs=[
                pl.BlockSpec((step, SEQ, HEAD), lambda i, x: (i, 0, 0)),
                pl.BlockSpec((docs, 3, SEQ, HEAD), lambda i, x: (0, 0, 0, 0)),
                pl.BlockSpec((docs, 1, docs * SEQ), lambda i, x: (0, 0, 0)),
            ],
            out_specs=[
                pl.BlockSpec((step, 2 * SEQ + 32, HEAD), lambda i, x: (i, 0, 0)),
                pl.BlockSpec((step, SEQ + 32, HEAD), lambda i, x: (i, 0, 0)),
            ],
            scratch_shapes=[
                pltpu.VMEM((docs * SEQ, HEAD), BF),
                pltpu.VMEM((docs * SEQ, HEAD), BF),
                pltpu.VMEM((docs * SEQ, 2 * HEAD), BF),
            ],
        ),
        out_shape=[
            jax.ShapeDtypeStruct((some, 2 * SEQ + 32, HEAD), BF),
            jax.ShapeDtypeStruct((some, SEQ + 32, HEAD), BF),
        ],
        compiler_params=pltpu.CompilerParams(vmem_limit_bytes=40 * 2**20),
        cost_estimate=pl.CostEstimate(
            flops=some * SEQ * SEQ, bytes_accessed=2**16, transcendentals=0
        ),
        name="cross",
    )(idx, q_heads, kvg, bias)


def by_heads_kernel(*refs):
    out_ref = refs[3]
    for c in range(4):
        for i in range(3):
            out_ref[c, i] = refs[i][0, :, c * HEAD : (c + 1) * HEAD]


def by_heads(*arrays):
    block = pl.BlockSpec((1, SEQ, 4 * HEAD), lambda i: (0, 0, i))
    return pl.pallas_call(
        by_heads_kernel,
        grid=(4,),
        in_specs=[block] * 3,
        out_specs=pl.BlockSpec((4, 3, SEQ, HEAD), lambda i: (i, 0, 0, 0)),
        out_shape=jax.ShapeDtypeStruct((HEADS, 3, SEQ, HEAD), BF),
        cost_estimate=pl.CostEstimate(flops=0, bytes_accessed=3 * 2**20, transcendentals=0),
        name="by_heads",
    )(*arrays)


def own_kernel(
    idx_ref, q_ref, g_ref, ck_ref, cv_ref, lk_ref, lv_ref, ab_ref, o_ref, s_ref
):
    cache = ck_ref.shape[1]
    entry = lax.broadcasted_iota(jnp.int32, (SEQ, cache), 1)
    row = lax.broadcasted_iota(jnp.int32, (SEQ, SEQ), 0)
    col = lax.broadcasted_iota(jnp.int32, (SEQ, SEQ), 1)
    for c in range(4):
        cols = slice(c * HEAD, (c + 1) * HEAD)
        k = idx_ref[1] ^ c
        q = q_ref[k]
        g = g_ref[0, :, cols]
        ck, cv = ck_ref[0, :, cols], cv_ref[0, :, cols]
        lk, lv = lk_ref[0, :, cols], lv_ref[0, :, cols]
        stale = jnp.where(entry < idx_ref[2], dot_nt(q, ck) * (SCALING * LOG2E), NEG)
        local = jnp.where(col <= row, dot_nt(q, lk) * (SCALING * LOG2E), NEG)
        top = jnp.maximum(
            jnp.max(stale, axis=1, keepdims=True), jnp.max(local, axis=1, keepdims=True)
        )
        ws = jnp.exp2(stale - top).astype(BF)
        wl = jnp.exp2(local - top).astype(BF)
        ws32 = ws.astype(F32)
        wl32 = wl.astype(F32)
        total = jnp.sum(ws32, axis=1, keepdims=True) + jnp.sum(wl32, axis=1, keepdims=True)
        inverse = 1.0 / total
        o = (dot_nn(ws, cv) + dot_nn(wl, lv)) * inverse
        b = (dot_nn(ws, ck) + dot_nn(wl, lk)) * inverse
        delta = jnp.sum(o * g.astype(F32), axis=1, keepdims=True)
        ss = (ws32 * (dot_nt(g, cv) - delta)).astype(BF)
        sl = (wl32 * (dot_nt(g, lv) - delta)).astype(BF)
        a = (dot_nn(ss, ck) + dot_nn(sl, lk)) * inverse
        rows = stat_rows([top, total, delta])[0:8, :]
        ab_ref[k, 0:SEQ, :] = a.astype(BF)
        ab_ref[k, SEQ : 2 * SEQ, :] = b.astype(BF)
        ab_ref[k, 2 * SEQ : 2 * SEQ + 32, :] = pack_rows(rows)
        o_ref[:, cols] = o
        s_ref[c] = rows


def own_attention(idx, q_own, grad, cache_k, cache_v, local_k, local_v):
    cache = cache_k.shape[1]
    width = HEADS * HEAD
    head_block = pl.BlockSpec((1, SEQ, 4 * HEAD), lambda j, x: (0, 0, (x[0] + j) % 4))
    cache_block = pl.BlockSpec((1, cache, 4 * HEAD), lambda j, x: (0, 0, (x[0] + j) % 4))
    return pl.pallas_call(
        own_kernel,
        grid_spec=pltpu.PrefetchScalarGridSpec(
            num_scalar_prefetch=1,
            grid=(4,),
            in_specs=[
                pl.BlockSpec((4, SEQ, HEAD), lambda j, x: (0, 0, j)),
                head_block,
                cache_block,
                cache_block,
                head_block,
                head_block,
            ],
            out_specs=[
                pl.BlockSpec((4, 2 * SEQ + 32, HEAD), lambda j, x: (0, 0, j)),
                pl.BlockSpec((SEQ, 4 * HEAD), lambda j, x: (0, (x[0] + j) % 4)),
                pl.BlockSpec((4, 8, SEQ), lambda j, x: ((x[0] + j) % 4, 0, 0)),
            ],
        ),
        out_shape=[
            jax.ShapeDtypeStruct((4, 2 * SEQ + 32, 4 * HEAD), BF),
            jax.ShapeDtypeStruct((SEQ, width), F32),
            jax.ShapeDtypeStruct((HEADS, 8, SEQ), F32),
        ],
        compiler_params=pltpu.CompilerParams(vmem_limit_bytes=24 * 2**20),
        cost_estimate=pl.CostEstimate(
            flops=cache * SEQ, bytes_accessed=2**16, transcendentals=0
        ),
        name="own",
    )(idx, q_own, grad, cache_k, cache_v, local_k, local_v)


def merge_rows(x_top, x_total, x_delta, o_top, o_total, o_delta):
    big = jnp.maximum(x_top, o_top)
    x_share = jnp.exp2(x_top - big)
    o_share = jnp.exp2(o_top - big)
    inverse = 1.0 / (x_share * x_total + o_share * o_total)
    x_weight = x_share * x_total * inverse
    o_weight = o_share * o_total * inverse
    delta = x_weight * x_delta + o_weight * o_delta
    return x_weight, o_weight, delta, o_share * inverse


def dest_kernel(*refs):
    x_refs, y_refs, qg_ref = refs[0:4], refs[4:8], refs[8]
    base = 2 * SEQ
    xs = [unpack_rows(x_refs[j][k, base : base + 32, :]) for k in range(4) for j in range(4)]
    ys = [
        unpack_rows(y_refs[k][base : base + 32, j * HEAD : (j + 1) * HEAD])
        for k in range(4)
        for j in range(4)
    ]
    x_stat = [jnp.concatenate([t[i : i + 1] for t in xs], axis=0) for i in range(3)]
    y_stat = [jnp.concatenate([t[i : i + 1] for t in ys], axis=0) for i in range(3)]
    x_weight, o_weight, delta, _ = merge_rows(*x_stat, *y_stat)
    rows = [
        x_weight * SCALING,
        x_weight * (x_stat[2] - delta) * SCALING,
        o_weight * SCALING,
        o_weight * (y_stat[2] - delta) * SCALING,
    ]
    tile = jnp.concatenate([*rows, jnp.zeros((SEQ - 64, SEQ), F32)], axis=0).T
    for k in range(4):
        for j in range(4):
            c = k * 4 + j
            cols = slice(j * HEAD, (j + 1) * HEAD)
            grad = (
                tile[:, c : c + 1] * x_refs[j][k, 0:SEQ, :].astype(F32)
                + tile[:, 16 + c : 17 + c] * x_refs[j][k, SEQ:base, :].astype(F32)
                + tile[:, 32 + c : 33 + c] * y_refs[k][0:SEQ, cols].astype(F32)
                + tile[:, 48 + c : 49 + c] * y_refs[k][SEQ:base, cols].astype(F32)
            )
            qg_ref[k * SEQ : (k + 1) * SEQ, cols] = grad.astype(BF)


def dest_combine(xs, ys):
    return pl.pallas_call(
        dest_kernel,
        out_shape=jax.ShapeDtypeStruct((4 * SEQ, 4 * HEAD), BF),
        compiler_params=pltpu.CompilerParams(vmem_limit_bytes=24 * 2**20),
        cost_estimate=pl.CostEstimate(
            flops=8 * 16 * SEQ * HEAD, bytes_accessed=3 * 2**20, transcendentals=0
        ),
        name="dest",
    )(*xs, *ys)


def finish_kernel(
    idx_ref, x_ref, o_ref, s_ref, q_ref, g_ref, lk_ref, lv_ref, att_ref, kg_ref, vg_ref
):
    key = lax.broadcasted_iota(jnp.int32, (SEQ, SEQ), 0)
    query = lax.broadcasted_iota(jnp.int32, (SEQ, SEQ), 1)
    for c in range(4):
        cols = slice(c * HEAD, (c + 1) * HEAD)
        k = idx_ref[1] ^ c
        q = q_ref[k]
        g = g_ref[0, :, cols]
        xr = unpack_rows(x_ref[k, 0, SEQ : SEQ + 32, :])
        yr = s_ref[c]
        x_weight, o_weight, delta, factor = merge_rows(
            xr[0:1], xr[1:2], xr[2:3], yr[0:1], yr[1:2], yr[2:3]
        )
        pair = jnp.concatenate([x_weight, o_weight, jnp.zeros((SEQ - 2, SEQ), F32)], axis=0).T
        att_ref[0, :, cols] = (
            pair[:, 0:1] * x_ref[k, 0, 0:SEQ, :].astype(F32) + pair[:, 1:2] * o_ref[:, cols]
        ).astype(BF)
        scores = dot_nt(lk_ref[0, :, cols], q) * (SCALING * LOG2E)
        scores = jnp.where(key <= query, scores, NEG)
        prob = jnp.exp2(scores - yr[0:1]).astype(BF).astype(F32) * factor
        slope = (prob * (dot_nt(lv_ref[0, :, cols], g) - delta)).astype(BF)
        vg_ref[0, :, cols] = dot_nn(prob.astype(BF), g).astype(BF)
        kg_ref[0, :, cols] = (dot_nn(slope, q) * SCALING).astype(BF)


def finish(idx, returned, o, stats, q_own, grad, local_k, local_v):
    width = HEADS * HEAD
    row_block = pl.BlockSpec((1, SEQ, 4 * HEAD), lambda i, x: (0, 0, i))
    return pl.pallas_call(
        finish_kernel,
        grid_spec=pltpu.PrefetchScalarGridSpec(
            num_scalar_prefetch=1,
            grid=(4,),
            in_specs=[
                pl.BlockSpec((4, 1, SEQ + 32, HEAD), lambda i, x: (0, (i + 4 - x[0]) % 4, 0, 0)),
                pl.BlockSpec((SEQ, 4 * HEAD), lambda i, x: (0, i)),
                pl.BlockSpec((4, 8, SEQ), lambda i, x: (i, 0, 0)),
                pl.BlockSpec((4, SEQ, HEAD), lambda i, x: (0, 0, (i + 4 - x[0]) % 4)),
                row_block,
                row_block,
                row_block,
            ],
            out_specs=[row_block, row_block, row_block],
        ),
        out_shape=[jax.ShapeDtypeStruct((1, SEQ, width), BF)] * 3,
        compiler_params=pltpu.CompilerParams(vmem_limit_bytes=24 * 2**20),
        cost_estimate=pl.CostEstimate(
            flops=10 * SEQ * SEQ * width,
            bytes_accessed=5 * 2**20,
            transcendentals=SEQ * SEQ * HEADS,
        ),
        name="finish",
    )(idx, returned, o, stats, q_own, grad, local_k, local_v)


def place_kernel(idx_ref, *refs):
    out_ref = refs[4]
    for k in range(4):
        for j in range(4):
            head = 4 * ((idx_ref[0] + j) % 4) + (idx_ref[1] ^ k)
            start = pl.multiple_of(head * HEAD, HEAD)
            out_ref[:, pl.ds(start, HEAD)] = refs[k][:, j * HEAD : (j + 1) * HEAD].astype(F32)


def place(idx, parts):
    rows = parts[0].shape[0]
    return pl.pallas_call(
        place_kernel,
        in_specs=[pl.BlockSpec(memory_space=pltpu.SMEM)] + [pl.BlockSpec()] * 4,
        out_shape=jax.ShapeDtypeStruct((rows, HEADS * HEAD), F32),
        cost_estimate=pl.CostEstimate(flops=0, bytes_accessed=2 * 2**20, transcendentals=0),
        name="place",
    )(idx, *parts)


def a2a(x, axis):
    return lax.all_to_all(x, axis, 0, 0, tiled=True)


def shift(x, axis, k):
    return lax.ppermute(x, axis, [(s, (s + k) % 4) for s in range(4)]) if k % 4 else x


def swap(x, axis, k):
    return lax.ppermute(x, axis, [(s, s ^ k) for s in range(4)]) if k else x


def in_order(mine, other, first, axis):
    return jnp.stack([jnp.where(first, mine, other), jnp.where(first, other, mine)], axis=axis)


def gather_shards(shard, tok1, tok2):
    x_index = lax.axis_index("x")
    slots = jnp.stack([shift(shard, "x", -k) for k in range(4)])
    slots = jnp.where(x_index % 2 == 1, jnp.roll(slots, 1, axis=0), slots)
    slots = jnp.where(x_index >= 2, jnp.roll(slots, 2, axis=0), slots)
    slots, tok1, tok2 = lax.optimization_barrier((slots, tok1, tok2))
    tok3 = swap(tok2, "q", 1)
    other = lax.ppermute(slots, "yh", [(0, 1), (1, 0)])
    slots = in_order(slots, other, lax.axis_index("yh") == 0, 1)
    slots, tok3 = lax.optimization_barrier((slots, tok3))
    other = lax.ppermute(slots, "core", [(0, 1), (1, 0)])
    slots = in_order(slots, other, lax.axis_index("core") == 0, 2)
    return slots.reshape(16 * shard.shape[0], -1), tok1, tok2, tok3


def body(
    tokens,
    query_weight,
    current_keys,
    current_values,
    cache_keys,
    cache_values,
    cache_fill,
    document_group,
    attended_grad,
):
    g_index = lax.axis_index("g")
    q_index = lax.axis_index("q")
    col_index = lax.axis_index(FS)
    idx = jnp.stack([g_index, q_index, cache_fill[0]]).astype(jnp.int32)

    own_tok = tokens[0]
    tok2, tok1 = swap(own_tok, "q", 2), swap(own_tok, "q", 1)
    kvg = by_heads(current_keys, current_values, attended_grad)
    quarter = jnp.concatenate(
        [
            lax.dynamic_slice_in_dim(
                query_weight, (4 * ((g_index + j) % 4) + q_index) * HEAD, HEAD, axis=1
            )
            for j in range(4)
        ],
        axis=1,
    )
    weight, tok1, tok2, tok3 = gather_shards(quarter, tok1, tok2)

    kvg = a2a(kvg, XB)

    tok = jnp.concatenate([own_tok, tok1, tok2, tok3])
    queries = jnp.dot(tok, weight, preferred_element_type=F32).astype(BF)
    later, kvg = lax.optimization_barrier((queries, kvg))
    by_slot = [queries[:, j * HEAD : (j + 1) * HEAD] for j in range(4)]
    q_heads = [shift(by_slot[j], "g", j).reshape(4, SEQ, HEAD) for j in range(4)]
    q_own = jnp.stack([swap(later[k * SEQ : (k + 1) * SEQ], "q", k) for k in range(4)])

    labels = lax.dynamic_index_in_dim(
        document_group.reshape(16, 16), col_index, axis=1, keepdims=False
    )
    number = jnp.arange(16)
    valid = (labels[:, None] == labels[None, :]) & (number[:, None] != number[None, :])
    bias = jnp.repeat(jnp.where(valid, 0.0, NEG).astype(F32), SEQ, axis=1)[:, None, :]

    ab, out = [None] * 4, [None] * 4
    halves = ((2, 0), (1, 3))
    two = [jnp.concatenate([q_heads[j] for j in slots]) for slots in halves]

    def cross_half(n):
        both, outs = cross_attention(idx, two[n], kvg, bias, halves[n])
        for i, j in enumerate(halves[n]):
            ab[j], out[j] = both[4 * i : 4 * i + 4], outs[4 * i : 4 * i + 4]
        return both

    q_own, _ = lax.optimization_barrier((q_own, cross_half(0)))
    up, down = shift(ab[2][:2], "g", -1), shift(ab[2][2:], "g", 1)
    own_ab, o, stats = own_attention(
        idx, q_own, attended_grad, cache_keys, cache_values, current_keys, current_values
    )
    two[1], stats, up, down = lax.optimization_barrier((two[1], stats, up, down))
    up, down = shift(up, "g", -1), shift(down, "g", 1)
    xs = [ab[0], None, jnp.concatenate([up, down]), None]
    ys = [swap(own_ab[k], "q", k) for k in range(4)]
    cross_half(1)
    xs[1], xs[3] = shift(ab[1], "g", -1), shift(ab[3], "g", -3)
    qg = dest_combine(xs, ys)

    partial = lax.dot_general(
        tok, qg, (((0,), (0,)), ((), ())), preferred_element_type=F32
    ).astype(BF)
    pieces = a2a(partial.reshape(16, query_weight.shape[0], 4 * HEAD), FS)
    mine = jnp.sum(pieces.astype(F32), axis=0).astype(BF)

    part = dot_nt(qg, weight).astype(BF).reshape(2, 2, SEQ, -1)
    swapped, _ = lax.optimization_barrier((swap(part[:, 1], "q", 1), mine))
    near = part[:, 0].astype(F32) + swapped.astype(F32)
    tokens_grad = near[0] + swap(near[1].astype(BF), "q", 2).astype(F32)
    tokens_grad = tokens_grad.astype(BF)[None]

    out, _ = lax.optimization_barrier((out, partial))
    over_g = [shift(out[j], "g", -j) for j in range(4)]
    over_g, _ = lax.optimization_barrier((over_g, mine))
    returned = jnp.stack(
        [swap(jnp.stack([over_g[j][k] for j in range(4)]), "q", k) for k in range(4)]
    )
    attended, keys_grad, values_grad = finish(
        idx, returned, o, stats, q_own, attended_grad, current_keys, current_values
    )

    summed = sum(
        jnp.roll(shift(mine, "g", k), -k * HEAD, axis=1).astype(F32) for k in range(4)
    ).astype(BF)
    weight_grad = place(idx, [swap(summed, "q", k) for k in range(4)])
    return attended, tokens_grad, keys_grad, values_grad, weight_grad


def solution(mesh):
    grid = Mesh(mesh.devices.reshape(4, 4, 4, 2, 2), XB + FS)
    docs = P(XB + FS, None, None)
    in_specs = (docs, P(FS, None), docs, docs, docs, docs, P(XB + FS), P(), docs)
    out_specs = (docs, docs, docs, docs, P(FS, None))
    return jax.shard_map(body, mesh=grid, in_specs=in_specs, out_specs=out_specs, check_vma=False)
```

```python
import functools

import jax
import jax.numpy as jnp
from jax import lax
from jax.experimental import pallas as pl
from jax.experimental.pallas import tpu as pltpu
from jax.sharding import Mesh
from jax.sharding import PartitionSpec as P

HEADS = 16
HEAD = 128
SEQ = 128
NEG = -1e30
FLOOR = -1e29
SCALING = HEAD ** (-0.5)
LOG2E = 1.4426950408889634
XB = ("g", "q")
FS = ("x", "yh", "core")
BF = jnp.bfloat16
F32 = jnp.float32


def dot_nt(a, b):
    return lax.dot_general(a, b, (((1,), (1,)), ((), ())), preferred_element_type=F32)


def dot_nn(a, b):
    return lax.dot_general(a, b, (((1,), (0,)), ((), ())), preferred_element_type=F32)


def split3(x):
    hi = x.astype(BF)
    rest = x - hi.astype(F32)
    mid = rest.astype(BF)
    low = (rest - mid.astype(F32)).astype(BF)
    return hi, mid, low


def stat_rows(columns):
    lane = lax.broadcasted_iota(jnp.int32, (SEQ, SEQ), 1)
    tile = jnp.zeros((SEQ, SEQ), F32)
    for i, column in enumerate(columns):
        tile = jnp.where(lane == i, column, tile)
    return tile.T


def pack_rows(rows):
    hi, mid, low = split3(rows)
    blank = jnp.zeros((8, SEQ), F32)
    parts = [hi.astype(F32), mid.astype(F32), low.astype(F32), blank]
    return jnp.concatenate(parts, axis=0).astype(BF)


def unpack_rows(packed):
    x = packed.astype(F32)
    return x[0:8] + x[8:16] + x[16:24]


def cross_kernel(idx_ref, q_ref, kvg_ref, bias_ref, ab_ref, o_ref, k_s, v_s, kv_s, *, slots):
    docs = kvg_ref.shape[0]
    step = q_ref.shape[0]

    @pl.when(pl.program_id(0) == 0)
    def _():
        for m in range(docs):
            k = kvg_ref[m, 0]
            v = kvg_ref[m, 1]
            k_s[m * SEQ : (m + 1) * SEQ, :] = k
            v_s[m * SEQ : (m + 1) * SEQ, :] = v
            kv_s[m * SEQ : (m + 1) * SEQ, :HEAD] = v
            kv_s[m * SEQ : (m + 1) * SEQ, HEAD:] = k

    first = pl.program_id(0) * step
    slot = jnp.where(first < 4, slots[0], slots[1])
    docs_at = [
        4 * ((idx_ref[0] + 4 - slot) % 4) + (idx_ref[1] ^ ((first + j) % 4)) for j in range(step)
    ]
    q = q_ref[...].reshape(step * SEQ, HEAD)
    g = jnp.concatenate([kvg_ref[doc, 2] for doc in docs_at], axis=0)
    scores = dot_nt(q, k_s[...]) * (SCALING * LOG2E)
    scores = jnp.concatenate(
        [scores[j * SEQ : (j + 1) * SEQ] + bias_ref[docs_at[j]] for j in range(step)], axis=0
    )
    top = jnp.maximum(jnp.max(scores, axis=1, keepdims=True), FLOOR)
    weights = jnp.exp2(scores - top).astype(BF)
    weights32 = weights.astype(F32)
    total = jnp.sum(weights32, axis=1, keepdims=True)
    inverse = 1.0 / jnp.maximum(total, 0.5)
    both = dot_nn(weights, kv_s[...]) * inverse
    o = both[:, :HEAD]
    delta = jnp.sum(o * g.astype(F32), axis=1, keepdims=True)
    slope = (weights32 * (dot_nt(g, v_s[...]) - delta)).astype(BF)
    a = dot_nn(slope, k_s[...]) * inverse
    top = jnp.where(total > 0.0, top, NEG)
    for j in range(step):
        rows = slice(j * SEQ, (j + 1) * SEQ)
        packed = pack_rows(stat_rows([top[rows], total[rows], delta[rows]])[0:8, :])
        ab_ref[j, 0:SEQ, :] = a[rows].astype(BF)
        ab_ref[j, SEQ : 2 * SEQ, :] = both[rows, HEAD:].astype(BF)
        ab_ref[j, 2 * SEQ : 2 * SEQ + 32, :] = packed
        o_ref[j, 0:SEQ, :] = o[rows].astype(BF)
        o_ref[j, SEQ : SEQ + 32, :] = packed


def cross_attention(idx, q_heads, kvg, bias, slots):
    docs = kvg.shape[0]
    some = q_heads.shape[0]
    step = 2
    return pl.pallas_call(
        functools.partial(cross_kernel, slots=slots),
        grid_spec=pltpu.PrefetchScalarGridSpec(
            num_scalar_prefetch=1,
            grid=(some // step,),
            in_specs=[
                pl.BlockSpec((step, SEQ, HEAD), lambda i, x: (i, 0, 0)),
                pl.BlockSpec((docs, 3, SEQ, HEAD), lambda i, x: (0, 0, 0, 0)),
                pl.BlockSpec((docs, 1, docs * SEQ), lambda i, x: (0, 0, 0)),
            ],
            out_specs=[
                pl.BlockSpec((step, 2 * SEQ + 32, HEAD), lambda i, x: (i, 0, 0)),
                pl.BlockSpec((step, SEQ + 32, HEAD), lambda i, x: (i, 0, 0)),
            ],
            scratch_shapes=[
                pltpu.VMEM((docs * SEQ, HEAD), BF),
                pltpu.VMEM((docs * SEQ, HEAD), BF),
                pltpu.VMEM((docs * SEQ, 2 * HEAD), BF),
            ],
        ),
        out_shape=[
            jax.ShapeDtypeStruct((some, 2 * SEQ + 32, HEAD), BF),
            jax.ShapeDtypeStruct((some, SEQ + 32, HEAD), BF),
        ],
        compiler_params=pltpu.CompilerParams(vmem_limit_bytes=40 * 2**20),
        cost_estimate=pl.CostEstimate(
            flops=some * SEQ * SEQ, bytes_accessed=2**16, transcendentals=0
        ),
        name="cross",
    )(idx, q_heads, kvg, bias)


def by_heads_kernel(*refs):
    out_ref = refs[3]
    for c in range(4):
        for i in range(3):
            out_ref[c, i] = refs[i][0, :, c * HEAD : (c + 1) * HEAD]


def by_heads(*arrays):
    block = pl.BlockSpec((1, SEQ, 4 * HEAD), lambda i: (0, 0, i))
    return pl.pallas_call(
        by_heads_kernel,
        grid=(4,),
        in_specs=[block] * 3,
        out_specs=pl.BlockSpec((4, 3, SEQ, HEAD), lambda i: (i, 0, 0, 0)),
        out_shape=jax.ShapeDtypeStruct((HEADS, 3, SEQ, HEAD), BF),
        cost_estimate=pl.CostEstimate(flops=0, bytes_accessed=3 * 2**20, transcendentals=0),
        name="by_heads",
    )(*arrays)


def own_kernel(
    idx_ref, q_ref, g_ref, ck_ref, cv_ref, lk_ref, lv_ref, ab_ref, o_ref, s_ref
):
    cache = ck_ref.shape[1]
    entry = lax.broadcasted_iota(jnp.int32, (SEQ, cache), 1)
    row = lax.broadcasted_iota(jnp.int32, (SEQ, SEQ), 0)
    col = lax.broadcasted_iota(jnp.int32, (SEQ, SEQ), 1)
    for c in range(4):
        cols = slice(c * HEAD, (c + 1) * HEAD)
        k = idx_ref[1] ^ c
        q = q_ref[k]
        g = g_ref[0, :, cols]
        ck, cv = ck_ref[0, :, cols], cv_ref[0, :, cols]
        lk, lv = lk_ref[0, :, cols], lv_ref[0, :, cols]
        stale = jnp.where(entry < idx_ref[2], dot_nt(q, ck) * (SCALING * LOG2E), NEG)
        local = jnp.where(col <= row, dot_nt(q, lk) * (SCALING * LOG2E), NEG)
        top = jnp.maximum(
            jnp.max(stale, axis=1, keepdims=True), jnp.max(local, axis=1, keepdims=True)
        )
        ws = jnp.exp2(stale - top).astype(BF)
        wl = jnp.exp2(local - top).astype(BF)
        ws32 = ws.astype(F32)
        wl32 = wl.astype(F32)
        total = jnp.sum(ws32, axis=1, keepdims=True) + jnp.sum(wl32, axis=1, keepdims=True)
        inverse = 1.0 / total
        o = (dot_nn(ws, cv) + dot_nn(wl, lv)) * inverse
        b = (dot_nn(ws, ck) + dot_nn(wl, lk)) * inverse
        delta = jnp.sum(o * g.astype(F32), axis=1, keepdims=True)
        ss = (ws32 * (dot_nt(g, cv) - delta)).astype(BF)
        sl = (wl32 * (dot_nt(g, lv) - delta)).astype(BF)
        a = (dot_nn(ss, ck) + dot_nn(sl, lk)) * inverse
        rows = stat_rows([top, total, delta])[0:8, :]
        ab_ref[k, 0:SEQ, :] = a.astype(BF)
        ab_ref[k, SEQ : 2 * SEQ, :] = b.astype(BF)
        ab_ref[k, 2 * SEQ : 2 * SEQ + 32, :] = pack_rows(rows)
        o_ref[:, cols] = o
        s_ref[c] = rows


def own_attention(idx, q_own, grad, cache_k, cache_v, local_k, local_v):
    cache = cache_k.shape[1]
    width = HEADS * HEAD
    head_block = pl.BlockSpec((1, SEQ, 4 * HEAD), lambda j, x: (0, 0, (x[0] + j) % 4))
    cache_block = pl.BlockSpec((1, cache, 4 * HEAD), lambda j, x: (0, 0, (x[0] + j) % 4))
    return pl.pallas_call(
        own_kernel,
        grid_spec=pltpu.PrefetchScalarGridSpec(
            num_scalar_prefetch=1,
            grid=(4,),
            in_specs=[
                pl.BlockSpec((4, SEQ, HEAD), lambda j, x: (0, 0, j)),
                head_block,
                cache_block,
                cache_block,
                head_block,
                head_block,
            ],
            out_specs=[
                pl.BlockSpec((4, 2 * SEQ + 32, HEAD), lambda j, x: (0, 0, j)),
                pl.BlockSpec((SEQ, 4 * HEAD), lambda j, x: (0, (x[0] + j) % 4)),
                pl.BlockSpec((4, 8, SEQ), lambda j, x: ((x[0] + j) % 4, 0, 0)),
            ],
        ),
        out_shape=[
            jax.ShapeDtypeStruct((4, 2 * SEQ + 32, 4 * HEAD), BF),
            jax.ShapeDtypeStruct((SEQ, width), F32),
            jax.ShapeDtypeStruct((HEADS, 8, SEQ), F32),
        ],
        compiler_params=pltpu.CompilerParams(vmem_limit_bytes=24 * 2**20),
        cost_estimate=pl.CostEstimate(
            flops=cache * SEQ, bytes_accessed=2**16, transcendentals=0
        ),
        name="own",
    )(idx, q_own, grad, cache_k, cache_v, local_k, local_v)


def merge_rows(x_top, x_total, x_delta, o_top, o_total, o_delta):
    big = jnp.maximum(x_top, o_top)
    x_share = jnp.exp2(x_top - big)
    o_share = jnp.exp2(o_top - big)
    inverse = 1.0 / (x_share * x_total + o_share * o_total)
    x_weight = x_share * x_total * inverse
    o_weight = o_share * o_total * inverse
    delta = x_weight * x_delta + o_weight * o_delta
    return x_weight, o_weight, delta, o_share * inverse


def dest_kernel(*refs):
    x_refs, y_refs, qg_ref = refs[0:4], refs[4:8], refs[8]
    base = 2 * SEQ
    xs = [unpack_rows(x_refs[j][k, base : base + 32, :]) for k in range(4) for j in range(4)]
    ys = [
        unpack_rows(y_refs[k][base : base + 32, j * HEAD : (j + 1) * HEAD])
        for k in range(4)
        for j in range(4)
    ]
    x_stat = [jnp.concatenate([t[i : i + 1] for t in xs], axis=0) for i in range(3)]
    y_stat = [jnp.concatenate([t[i : i + 1] for t in ys], axis=0) for i in range(3)]
    x_weight, o_weight, delta, _ = merge_rows(*x_stat, *y_stat)
    rows = [
        x_weight * SCALING,
        x_weight * (x_stat[2] - delta) * SCALING,
        o_weight * SCALING,
        o_weight * (y_stat[2] - delta) * SCALING,
    ]
    tile = jnp.concatenate([*rows, jnp.zeros((SEQ - 64, SEQ), F32)], axis=0).T
    for k in range(4):
        for j in range(4):
            c = k * 4 + j
            cols = slice(j * HEAD, (j + 1) * HEAD)
            grad = (
                tile[:, c : c + 1] * x_refs[j][k, 0:SEQ, :].astype(F32)
                + tile[:, 16 + c : 17 + c] * x_refs[j][k, SEQ:base, :].astype(F32)
                + tile[:, 32 + c : 33 + c] * y_refs[k][0:SEQ, cols].astype(F32)
                + tile[:, 48 + c : 49 + c] * y_refs[k][SEQ:base, cols].astype(F32)
            )
            qg_ref[k * SEQ : (k + 1) * SEQ, cols] = grad.astype(BF)


def dest_combine(xs, ys):
    return pl.pallas_call(
        dest_kernel,
        out_shape=jax.ShapeDtypeStruct((4 * SEQ, 4 * HEAD), BF),
        compiler_params=pltpu.CompilerParams(vmem_limit_bytes=24 * 2**20),
        cost_estimate=pl.CostEstimate(
            flops=8 * 16 * SEQ * HEAD, bytes_accessed=3 * 2**20, transcendentals=0
        ),
        name="dest",
    )(*xs, *ys)


def finish_kernel(
    idx_ref, x_ref, o_ref, s_ref, q_ref, g_ref, lk_ref, lv_ref, att_ref, kg_ref, vg_ref
):
    key = lax.broadcasted_iota(jnp.int32, (SEQ, SEQ), 0)
    query = lax.broadcasted_iota(jnp.int32, (SEQ, SEQ), 1)
    for c in range(4):
        cols = slice(c * HEAD, (c + 1) * HEAD)
        k = idx_ref[1] ^ c
        q = q_ref[k]
        g = g_ref[0, :, cols]
        xr = unpack_rows(x_ref[k, 0, SEQ : SEQ + 32, :])
        yr = s_ref[c]
        x_weight, o_weight, delta, factor = merge_rows(
            xr[0:1], xr[1:2], xr[2:3], yr[0:1], yr[1:2], yr[2:3]
        )
        pair = jnp.concatenate([x_weight, o_weight, jnp.zeros((SEQ - 2, SEQ), F32)], axis=0).T
        att_ref[0, :, cols] = (
            pair[:, 0:1] * x_ref[k, 0, 0:SEQ, :].astype(F32) + pair[:, 1:2] * o_ref[:, cols]
        ).astype(BF)
        scores = dot_nt(lk_ref[0, :, cols], q) * (SCALING * LOG2E)
        scores = jnp.where(key <= query, scores, NEG)
        prob = jnp.exp2(scores - yr[0:1]).astype(BF).astype(F32) * factor
        slope = (prob * (dot_nt(lv_ref[0, :, cols], g) - delta)).astype(BF)
        vg_ref[0, :, cols] = dot_nn(prob.astype(BF), g).astype(BF)
        kg_ref[0, :, cols] = (dot_nn(slope, q) * SCALING).astype(BF)


def finish(idx, returned, o, stats, q_own, grad, local_k, local_v):
    width = HEADS * HEAD
    row_block = pl.BlockSpec((1, SEQ, 4 * HEAD), lambda i, x: (0, 0, i))
    return pl.pallas_call(
        finish_kernel,
        grid_spec=pltpu.PrefetchScalarGridSpec(
            num_scalar_prefetch=1,
            grid=(4,),
            in_specs=[
                pl.BlockSpec((4, 1, SEQ + 32, HEAD), lambda i, x: (0, (i + 4 - x[0]) % 4, 0, 0)),
                pl.BlockSpec((SEQ, 4 * HEAD), lambda i, x: (0, i)),
                pl.BlockSpec((4, 8, SEQ), lambda i, x: (i, 0, 0)),
                pl.BlockSpec((4, SEQ, HEAD), lambda i, x: (0, 0, (i + 4 - x[0]) % 4)),
                row_block,
                row_block,
                row_block,
            ],
            out_specs=[row_block, row_block, row_block],
        ),
        out_shape=[jax.ShapeDtypeStruct((1, SEQ, width), BF)] * 3,
        compiler_params=pltpu.CompilerParams(vmem_limit_bytes=24 * 2**20),
        cost_estimate=pl.CostEstimate(
            flops=10 * SEQ * SEQ * width,
            bytes_accessed=5 * 2**20,
            transcendentals=SEQ * SEQ * HEADS,
        ),
        name="finish",
    )(idx, returned, o, stats, q_own, grad, local_k, local_v)


def place_kernel(idx_ref, *refs):
    out_ref = refs[4]
    for k in range(4):
        for j in range(4):
            head = 4 * ((idx_ref[0] + j) % 4) + (idx_ref[1] ^ k)
            start = pl.multiple_of(head * HEAD, HEAD)
            out_ref[:, pl.ds(start, HEAD)] = refs[k][:, j * HEAD : (j + 1) * HEAD].astype(F32)


def place(idx, parts):
    rows = parts[0].shape[0]
    return pl.pallas_call(
        place_kernel,
        in_specs=[pl.BlockSpec(memory_space=pltpu.SMEM)] + [pl.BlockSpec()] * 4,
        out_shape=jax.ShapeDtypeStruct((rows, HEADS * HEAD), F32),
        cost_estimate=pl.CostEstimate(flops=0, bytes_accessed=2 * 2**20, transcendentals=0),
        name="place",
    )(idx, *parts)


def a2a(x, axis):
    return lax.all_to_all(x, axis, 0, 0, tiled=True)


def shift(x, axis, k):
    return lax.ppermute(x, axis, [(s, (s + k) % 4) for s in range(4)]) if k % 4 else x


def swap(x, axis, k):
    return lax.ppermute(x, axis, [(s, s ^ k) for s in range(4)]) if k else x


def in_order(mine, other, first, axis):
    return jnp.stack([jnp.where(first, mine, other), jnp.where(first, other, mine)], axis=axis)


def gather_shards(shard, tok1, tok2, kvg):
    x_index = lax.axis_index("x")
    slots = jnp.stack([shift(shard, "x", -k) for k in range(4)])
    slots = jnp.where(x_index % 2 == 1, jnp.roll(slots, 1, axis=0), slots)
    slots = jnp.where(x_index >= 2, jnp.roll(slots, 2, axis=0), slots)
    slots, tok1, tok2, _ = lax.optimization_barrier((slots, tok1, tok2, kvg))
    tok3 = swap(tok2, "q", 1)
    other = lax.ppermute(slots, "yh", [(0, 1), (1, 0)])
    slots = in_order(slots, other, lax.axis_index("yh") == 0, 1)
    slots, tok3 = lax.optimization_barrier((slots, tok3))
    other = lax.ppermute(slots, "core", [(0, 1), (1, 0)])
    slots = in_order(slots, other, lax.axis_index("core") == 0, 2)
    return slots.reshape(16 * shard.shape[0], -1), tok1, tok2, tok3


def body(
    tokens,
    query_weight,
    current_keys,
    current_values,
    cache_keys,
    cache_values,
    cache_fill,
    document_group,
    attended_grad,
):
    g_index = lax.axis_index("g")
    q_index = lax.axis_index("q")
    col_index = lax.axis_index(FS)
    idx = jnp.stack([g_index, q_index, cache_fill[0]]).astype(jnp.int32)

    own_tok = tokens[0]
    kvg = by_heads(current_keys, current_values, attended_grad)
    tok2, tok1 = swap(own_tok, "q", 2), swap(own_tok, "q", 1)
    quarter = jnp.concatenate(
        [
            lax.dynamic_slice_in_dim(
                query_weight, (4 * ((g_index + j) % 4) + q_index) * HEAD, HEAD, axis=1
            )
            for j in range(4)
        ],
        axis=1,
    )
    weight, tok1, tok2, tok3 = gather_shards(quarter, tok1, tok2, kvg)

    kvg = a2a(kvg, XB)

    tok = jnp.concatenate([own_tok, tok1, tok2, tok3])
    queries = jnp.dot(tok, weight, preferred_element_type=F32).astype(BF)
    later, kvg = lax.optimization_barrier((queries, kvg))
    by_slot = [queries[:, j * HEAD : (j + 1) * HEAD] for j in range(4)]
    q_heads = [shift(by_slot[j], "g", j).reshape(4, SEQ, HEAD) for j in range(4)]
    q_own = jnp.stack([swap(later[k * SEQ : (k + 1) * SEQ], "q", k) for k in range(4)])

    labels = lax.dynamic_index_in_dim(
        document_group.reshape(16, 16), col_index, axis=1, keepdims=False
    )
    number = jnp.arange(16)
    valid = (labels[:, None] == labels[None, :]) & (number[:, None] != number[None, :])
    bias = jnp.repeat(jnp.where(valid, 0.0, NEG).astype(F32), SEQ, axis=1)[:, None, :]

    ab, out = [None] * 4, [None] * 4
    halves = ((2, 0), (1, 3))
    two = [jnp.concatenate([q_heads[j] for j in slots]) for slots in halves]

    def cross_half(n):
        both, outs = cross_attention(idx, two[n], kvg, bias, halves[n])
        for i, j in enumerate(halves[n]):
            ab[j], out[j] = both[4 * i : 4 * i + 4], outs[4 * i : 4 * i + 4]
        return both

    q_own, _ = lax.optimization_barrier((q_own, cross_half(0)))
    up, down = shift(ab[2][:2], "g", -1), shift(ab[2][2:], "g", 1)
    own_ab, o, stats = own_attention(
        idx, q_own, attended_grad, cache_keys, cache_values, current_keys, current_values
    )
    two[1], stats, up, down = lax.optimization_barrier((two[1], stats, up, down))
    up, down = shift(up, "g", -1), shift(down, "g", 1)
    xs = [ab[0], None, jnp.concatenate([up, down]), None]
    ys = [swap(own_ab[k], "q", k) for k in range(4)]
    cross_half(1)
    xs[1], xs[3] = shift(ab[1], "g", -1), shift(ab[3], "g", -3)
    qg = dest_combine(xs, ys)

    partial = lax.dot_general(
        tok, qg, (((0,), (0,)), ((), ())), preferred_element_type=F32
    ).astype(BF)
    pieces = a2a(partial.reshape(16, query_weight.shape[0], 4 * HEAD), FS)
    mine = jnp.sum(pieces.astype(F32), axis=0).astype(BF)

    out, _ = lax.optimization_barrier((out, partial))
    over_g = [shift(out[j], "g", -j) for j in range(4)]
    over_g, _ = lax.optimization_barrier((over_g, mine))
    returned = jnp.stack(
        [swap(jnp.stack([over_g[j][k] for j in range(4)]), "q", k) for k in range(4)]
    )
    attended, keys_grad, values_grad = finish(
        idx, returned, o, stats, q_own, attended_grad, current_keys, current_values
    )

    summed = sum(
        jnp.roll(shift(mine, "g", k), -k * HEAD, axis=1).astype(F32) for k in range(4)
    ).astype(BF)

    part = dot_nt(qg, weight).astype(BF).reshape(2, 2, SEQ, -1)
    swapped, _ = lax.optimization_barrier((swap(part[:, 1], "q", 1), summed))
    near = part[:, 0].astype(F32) + swapped.astype(F32)
    tokens_grad = near[0] + swap(near[1].astype(BF), "q", 2).astype(F32)
    tokens_grad = tokens_grad.astype(BF)[None]

    weight_grad = place(idx, [swap(summed, "q", k) for k in range(4)])
    return attended, tokens_grad, keys_grad, values_grad, weight_grad


def solution(mesh):
    grid = Mesh(mesh.devices.reshape(4, 4, 4, 2, 2), XB + FS)
    docs = P(XB + FS, None, None)
    in_specs = (docs, P(FS, None), docs, docs, docs, docs, P(XB + FS), P(), docs)
    out_specs = (docs, docs, docs, docs, P(FS, None))
    return jax.shard_map(body, mesh=grid, in_specs=in_specs, out_specs=out_specs, check_vma=False)
```
